32 devices in a mesh: group: 8 (over z, x), expert: 4 (over y, core).
Axes of the slice: x: 2, y: 2, z: 4, core: 2. Of those that a mesh axis runs over, the one named last changes fastest.
Arguments:
- hidden_in: bfloat16 [8192, 2048], P(('group', 'expert')), may hold values from -54 to 54
- norm_attention: float32 [2048], replicated, may hold values from 0.5 to 1.5
- norm_experts: float32 [2048], replicated, may hold values from 0.5 to 1.5
- query_master: float32 [2048, 4096], P('group', 'expert'), may hold values from -0.125 to 0.125
- trainer_key_value_weight: float32 [2, 2048, 512], P(None, 'group'), may hold values from -0.125 to 0.125
- output_master: float32 [4096, 2048], P('expert', 'group'), may hold values from -0.09375 to 0.09375
- query_gain: float32 [128], replicated, may hold values from 0.5 to 1.5
- key_gain: float32 [128], replicated, may hold values from 0.5 to 1.5
- lengths: int32 [4], replicated, may hold values from 1 to 2048, as said below
- router: bfloat16 [2048, 128], replicated, may hold values from -0.125 to 0.125
- expert_gateup: bfloat16 [4, 2048, 1536], P('expert'), may hold values from -0.125 to 0.125
- expert_down: bfloat16 [4, 768, 2048], P('expert'), may hold values from -0.21875 to 0.21875
- routes: int32 [8192, 8], P(('group', 'expert')), may hold values from 0 to 127, as said below
Outputs:
- hidden: bfloat16 [8192, 2048], P(('group', 'expert'))
- expert_mix: bfloat16 [8192, 2048], P(('group', 'expert'))
The draws below stay inside these ranges and needn't reach their ends.
Inputs may be any that keep to these rules, and one draw needn't show every extreme that they name: `lengths`: one request has exactly 2048 valid tokens. `routes`: A row's 8 experts are different, and at most one of them is below 4. In the 256 rows of one device, each expert below 4 is named by at most 64 rows; in every such block some expert is named by exactly 64 rows, and one expert is named by exactly 64 rows in every block.
All inputs are finite; a program needn't handle non-finite values.
Results may differ from the reference program's by a relative error of at most 0.02.
Values may be sent and summed in bfloat16 or wider, within the bound.
No kernel may reach another device: no remote copies, remote signals or barrier semaphores. Data moves between devices by JAX's collectives and lax.ppermute only.
A program may use at most 128 MiB of HBM per device.

```python
import math
import jax
import jax.numpy as jnp
from jax import lax

MODEL_DIMENSION = 2048
QUERY_HEADS = 32
KEY_VALUE_HEADS = 4
HEAD_DIMENSION = 128
EXPERTS = 128
FFE = 768
TOPK = 8
SEQ_G = 1024
ROWS_DEV = 256
CAP = 64
EXPERTS_WIN = 4
PAIRS = 4
TOKENS = 8192
N_GROUP = 8
N_EXPERT = 4


def draw_hidden_in(key, part):
    subkeys = jax.random.split(key, 3)
    lowest = math.log(0.3)
    highest = math.log(3.0)
    row_scale = jnp.exp(jax.random.uniform(subkeys[0], (TOKENS, 1), jnp.float32, lowest, highest))
    column_scale = jnp.exp(jax.random.uniform(subkeys[1], (1, MODEL_DIMENSION), jnp.float32, lowest, highest))
    noise = jnp.clip(jax.random.normal(subkeys[2], (TOKENS, MODEL_DIMENSION), jnp.float32), -6.0, 6.0)
    return (noise * row_scale * column_scale).astype(jnp.bfloat16)


def draw_lengths(key, part):
    subkeys = jax.random.split(key, 2)
    drawn = jax.random.randint(subkeys[0], (PAIRS,), 1, 2 * SEQ_G + 1)
    longest = jax.random.randint(subkeys[1], (), 0, PAIRS)
    return jnp.where(jnp.arange(PAIRS) == longest, 2 * SEQ_G, drawn).astype(jnp.int32)


def draw_routes(key, part):
    subkeys = jax.random.split(key, 7)
    block_count = TOKENS // ROWS_DEV
    window = EXPERTS_WIN
    ceiling = jax.random.randint(subkeys[0], (window,), CAP // 2, CAP + 1)
    counts = ceiling[None, :] - jax.random.randint(subkeys[1], (block_count, window), 0, CAP // 2 + 1)
    busiest = jax.random.randint(subkeys[2], (block_count,), 0, window)
    hottest = jax.random.randint(subkeys[6], (), 0, window)
    columns = jnp.arange(window)[None, :]
    counts = jnp.where((columns == busiest[:, None]) | (columns == hottest), CAP, counts)
    bounds = jnp.cumsum(counts, axis=1)
    ranking = jax.vmap(lambda subkey: jax.random.permutation(subkey, ROWS_DEV))(jax.random.split(subkeys[3], block_count))
    chosen = jnp.sum((ranking[:, :, None] >= bounds[:, None, :]).astype(jnp.int32), axis=2).reshape(TOKENS)
    outside = EXPERTS - window
    scores = jax.random.randint(subkeys[4], (TOKENS, outside), 0, 1 << 20) * outside + jnp.arange(outside)[None, :]
    _, others = lax.top_k(scores, TOPK)
    others = others + window
    position = jax.random.randint(subkeys[5], (TOKENS, 1), 0, TOPK)
    place_here = (jnp.arange(TOPK)[None, :] == position) & (chosen[:, None] < window)
    return jnp.where(place_here, chosen[:, None], others).astype(jnp.int32)


def shard_levels(rng, extent, pieces, low, largest):
    level, own = 1.0, jax.random.fold_in(rng, 6)
    for dim, blocks in pieces:
        draws = jnp.exp(jax.random.uniform(jax.random.fold_in(own, dim), (blocks,), jnp.float32, low / len(pieces), largest / len(pieces)))
        level = level * jnp.repeat(draws, extent[dim] // blocks).reshape([-1 if axis == dim else 1 for axis in range(len(extent))])
    return level


def gaussian(own_key, dims, scale, reach, cuts=(), kind=jnp.bfloat16):
    array = scale * jax.random.normal(own_key, dims, jnp.float32)
    if cuts:
        array = array * shard_levels(own_key, dims, cuts, -0.22, 0.18)
    return jnp.clip(array, -reach, reach).astype(kind)


def setup_inputs(seed: int = 0) -> dict:
    key_list = jax.random.split(jax.random.key(seed), 14)
    return {
        "hidden_in": draw_hidden_in(jax.random.fold_in(key_list[13], 71), 0),
        "norm_attention": jnp.clip(jax.random.uniform(key_list[1], (MODEL_DIMENSION,), jnp.float32, 0.5, 1.5), 0.5, 1.5),
        "norm_experts": jnp.clip(jax.random.uniform(key_list[2], (MODEL_DIMENSION,), jnp.float32, 0.5, 1.5), 0.5, 1.5),
        "query_master": gaussian(key_list[3], (MODEL_DIMENSION, QUERY_HEADS * HEAD_DIMENSION), MODEL_DIMENSION ** -0.5, 0.125, ((0, 8), (1, 4)), jnp.float32),
        "trainer_key_value_weight": gaussian(key_list[4], (2, MODEL_DIMENSION, KEY_VALUE_HEADS * HEAD_DIMENSION), MODEL_DIMENSION ** -0.5, 0.125, ((1, 8),), jnp.float32),
        "output_master": gaussian(key_list[5], (QUERY_HEADS * HEAD_DIMENSION, MODEL_DIMENSION), (QUERY_HEADS * HEAD_DIMENSION) ** -0.5, 0.09375, ((0, 4), (1, 8)), jnp.float32),
        "query_gain": jnp.clip(jax.random.uniform(key_list[6], (HEAD_DIMENSION,), jnp.float32, 0.5, 1.5), 0.5, 1.5),
        "key_gain": jnp.clip(jax.random.uniform(key_list[7], (HEAD_DIMENSION,), jnp.float32, 0.5, 1.5), 0.5, 1.5),
        "lengths": draw_lengths(jax.random.fold_in(key_list[13], 71), 0),
        "router": gaussian(key_list[9], (MODEL_DIMENSION, EXPERTS), MODEL_DIMENSION ** -0.5, 0.125),
        "expert_gateup": gaussian(key_list[10], (EXPERTS_WIN, MODEL_DIMENSION, 2 * FFE), MODEL_DIMENSION ** -0.5, 0.125, ((0, 4),)),
        "expert_down": gaussian(key_list[11], (EXPERTS_WIN, FFE, MODEL_DIMENSION), FFE ** -0.5, 0.21875, ((0, 4),)),
        "routes": draw_routes(jax.random.fold_in(key_list[13], 71), 0),
    }


epsilon = 1e-06
rope_theta = 1000000.0

def norm_rows(values, gain_vector):
    widened = values.astype(jnp.float32)
    inverse_rms = lax.rsqrt(lax.optimization_barrier(jnp.mean(widened * widened, axis=-1, keepdims=True)) + epsilon)
    return widened * inverse_rms * gain_vector

def rotate(values, positions):
    half_width = values.shape[-1] // 2
    exponents = jnp.arange(half_width).astype(jnp.float32)
    inverse = jnp.exp(exponents * (-2.0 * math.log(rope_theta) / values.shape[-1]))
    angles = positions[:, None, None] * inverse[None, None, :]
    cosine_values = jnp.cos(angles)
    sine_values = jnp.sin(angles)
    first_half = values[..., :half_width]
    second = values[..., half_width:]
    return jnp.concatenate([first_half * cosine_values - second * sine_values, second * cosine_values + first_half * sine_values], axis=-1)

def local_positions(parity, row_count):
    indices = jnp.arange(row_count).astype(jnp.int32)
    quarter = row_count // 2
    offset = jnp.where(parity == 0, jnp.where(indices < quarter, 0, 2 * quarter), quarter)
    return indices + offset

def reference(hidden_in, norm_attention, norm_experts, query_master, trainer_key_value_weight, output_master, query_gain, key_gain, lengths, router, expert_gateup, expert_down, routes):
    query_weight = query_master.astype(jnp.bfloat16)
    key_matrix = trainer_key_value_weight[0].astype(jnp.bfloat16)
    value_matrix = trainer_key_value_weight[1].astype(jnp.bfloat16)
    output_weight = output_master.astype(jnp.bfloat16)
    normed = norm_rows(hidden_in, norm_attention).astype(jnp.bfloat16)
    group_member_count = QUERY_HEADS // KEY_VALUE_HEADS
    paired_rows = 2 * SEQ_G
    score_scale = HEAD_DIMENSION ** (-0.5)

    def one_pair(pair_index):
        paired_states = lax.dynamic_slice_in_dim(normed, pair_index * paired_rows, paired_rows, 0)
        query_rows_list = jnp.dot(paired_states, query_weight, preferred_element_type=jnp.float32).astype(jnp.bfloat16).reshape(paired_rows, QUERY_HEADS, HEAD_DIMENSION)
        paired_keys = jnp.dot(paired_states, key_matrix, preferred_element_type=jnp.float32).astype(jnp.bfloat16).reshape(paired_rows, KEY_VALUE_HEADS, HEAD_DIMENSION)
        paired_values = jnp.dot(paired_states, value_matrix, preferred_element_type=jnp.float32).astype(jnp.bfloat16).reshape(paired_rows, KEY_VALUE_HEADS, HEAD_DIMENSION)
        positions = jnp.concatenate([local_positions(0, SEQ_G), local_positions(1, SEQ_G)])
        places = positions.astype(jnp.float32)
        query_rows_list = rotate(norm_rows(query_rows_list, query_gain), places).astype(jnp.bfloat16)
        paired_keys = rotate(norm_rows(paired_keys, key_gain), places).astype(jnp.bfloat16)
        length = lengths[pair_index]
        allowed = (positions[None, :] <= positions[:, None]) & (positions[None, :] < length)
        query_broad = query_rows_list.astype(jnp.float32).reshape(paired_rows, KEY_VALUE_HEADS, group_member_count, HEAD_DIMENSION)
        key_wide = paired_keys.astype(jnp.float32)
        value_wide = paired_values.astype(jnp.float32)

        def single_group(head_index):
            query_head = lax.dynamic_index_in_dim(query_broad, head_index, 1, keepdims=False)
            key_head = lax.dynamic_index_in_dim(key_wide, head_index, 1, keepdims=False)
            value_head = lax.dynamic_index_in_dim(value_wide, head_index, 1, keepdims=False)
            scores = jnp.einsum('qgd,kd->gqk', query_head, key_head) * score_scale
            weights = jnp.where(allowed[None], jnp.exp(scores), 0.0)
            denominators = lax.optimization_barrier(jnp.sum(weights, axis=-1))
            rounded = lax.optimization_barrier(weights.astype(jnp.bfloat16)).astype(jnp.float32)
            output = jnp.einsum('gqk,kd->qgd', rounded, value_head) / jnp.transpose(denominators)[:, :, None]
            return output.astype(jnp.bfloat16)
        grouped_heads = lax.map(single_group, jnp.arange(KEY_VALUE_HEADS))
        return jnp.transpose(grouped_heads, (1, 0, 2, 3)).reshape(paired_rows, QUERY_HEADS * HEAD_DIMENSION)
    attended = lax.map(one_pair, jnp.arange(N_GROUP // 2)).reshape(TOKENS, QUERY_HEADS * HEAD_DIMENSION)
    block_width = QUERY_HEADS * HEAD_DIMENSION // N_EXPERT

    def add_block(total, block_index):
        columns = lax.dynamic_slice_in_dim(attended, block_index * block_width, block_width, 1)
        rows = lax.dynamic_slice_in_dim(output_weight, block_index * block_width, block_width, 0)
        partial_block = lax.optimization_barrier(jnp.dot(columns, rows, preferred_element_type=jnp.float32).astype(jnp.bfloat16)).astype(jnp.float32)
        return (total + partial_block, None)
    summed, _ = lax.scan(add_block, jnp.zeros((TOKENS, MODEL_DIMENSION), jnp.float32), jnp.arange(N_EXPERT))
    hidden = (hidden_in.astype(jnp.float32) + summed).astype(jnp.bfloat16)
    normed_second = norm_rows(hidden, norm_experts).astype(jnp.bfloat16)
    logits = jnp.dot(normed_second, router, preferred_element_type=jnp.float32)
    picked = jnp.take_along_axis(logits, routes, axis=1)
    raised = jnp.exp(picked)
    gate_values = raised / lax.optimization_barrier(jnp.sum(raised, axis=1, keepdims=True))
    inside = routes < EXPERTS_WIN
    gate_window = lax.optimization_barrier(jnp.sum(jnp.where(inside, gate_values, 0.0), axis=1))
    expert_window = lax.optimization_barrier(jnp.sum(jnp.where(inside, routes, 0), axis=1))
    present = jnp.any(inside, axis=1)
    slot_count = N_GROUP * N_EXPERT * CAP

    def one_expert(accumulated, expert):
        missing = jnp.where(present & (expert_window == expert), 0, 1).astype(jnp.int32)
        ordering = jnp.argsort(missing, stable=True)[:slot_count]
        chosen_rows = normed_second[ordering]
        gate_up = jnp.dot(chosen_rows, expert_gateup[expert], preferred_element_type=jnp.float32)
        active = (jax.nn.silu(gate_up[:, :FFE]) * gate_up[:, FFE:]).astype(jnp.bfloat16)
        output = lax.optimization_barrier(jnp.dot(active, expert_down[expert], preferred_element_type=jnp.float32).astype(jnp.bfloat16)).astype(jnp.float32)
        valid_slots = (missing[ordering] == 0)[:, None]
        accumulated = accumulated.at[ordering].add(jnp.where(valid_slots, output, 0.0))
        return (accumulated, None)
    combined, _ = lax.scan(one_expert, jnp.zeros((TOKENS, MODEL_DIMENSION), jnp.float32), jnp.arange(EXPERTS_WIN))
    expert_mix = (gate_window[:, None] * combined).astype(jnp.bfloat16)
    return (hidden, expert_mix)
```

```python
import functools
import math

import jax
import jax.numpy as jnp
from jax import lax
from jax.experimental import pallas as pl
from jax.experimental.pallas import tpu as pltpu
from jax.sharding import PartitionSpec as P

QUERY_HEADS = 32
KEY_VALUE_HEADS = 4
HEAD_DIMENSION = 128

epsilon = 1e-06
rope_theta = 1000000.0
VMEM_LIMIT = 56 * 1024 * 1024


def norm_rows(values, gain_vector):
    widened = values.astype(jnp.float32)
    inverse_rms = lax.rsqrt(jnp.mean(widened * widened, axis=-1, keepdims=True) + epsilon)
    return widened * inverse_rms * gain_vector


def local_positions(parity, row_count):
    indices = jnp.arange(row_count)
    quarter = row_count // 2
    offset = jnp.where(parity == 0, jnp.where(indices < quarter, 0, 2 * quarter), quarter)
    return indices + offset


def from_xor(block, axis, mask):
    count = lax.axis_size(axis)
    return lax.ppermute(block, axis, [(i, i ^ mask) for i in range(count)])


def gather_group(block):
    count = lax.axis_size("group")
    places = count // 2
    shards = {(0, 0): block}

    def cross(shard, step):
        route = [(i, i ^ 1) for i in range(count) if 0 <= i // 2 + step < places]
        return lax.ppermute(shard, "group", route)

    shards[1, 0] = cross(block, 0)
    above = below = block
    for step in range(1, places):
        above = lax.ppermute(above, "group", [(i, i - 2) for i in range(2, count)])
        below = lax.ppermute(below, "group", [(i, i + 2) for i in range(count - 2)])
        shards[0, step] = above
        shards[0, -step] = below
        shards[1, step] = cross(above, step)
        shards[1, -step] = cross(below, -step)
    return shards


def doubling_masks(count):
    masks, stride = [0], count // 2
    while stride:
        masks = masks + [mask ^ stride for mask in masks]
        stride //= 2
    return masks


def gather_tokens(rows):
    blocks = rows[None]
    stride = lax.axis_size("expert") // 2
    while stride:
        blocks = jnp.concatenate([blocks, from_xor(blocks, "expert", stride)], axis=0)
        stride //= 2
    return blocks


def scatter_sum(blocks):
    stride = 1
    while blocks.shape[0] > 1:
        half = blocks.shape[0] // 2
        arrived = from_xor(blocks[half:], "expert", stride)
        blocks = blocks[:half].astype(jnp.float32) + arrived.astype(jnp.float32)
        if half > 1:
            blocks = blocks.astype(jnp.bfloat16)
        stride *= 2
    return blocks[0]


def load_shards(place, side, places, keys, shard_refs, target, sem):
    for goal in range(places):
        for here in range(places):
            for offset in range(2):

                @pl.when(place == here)
                def _():
                    ref = shard_refs[keys.index((offset, goal - here))]
                    group = 2 * goal + (side ^ offset)
                    pltpu.make_async_copy(ref, target(group), sem).start()

    for group in range(2 * places):
        pltpu.make_async_copy(shard_refs[0], target(group), sem).wait()


def project_kernel(heads, places, keys, meta, rows, cosine, sine, gains, *rest):
    shard_refs = rest[: len(keys)]
    query_out, key_out, value_out, weights, sem = rest[len(keys) :]
    depth = shard_refs[0].shape[0]
    dim = HEAD_DIMENSION

    @pl.when(pl.program_id(0) == 0)
    def _():
        load_shards(
            meta[0], meta[1], places, keys, shard_refs,
            lambda group: weights.at[pl.ds(pl.multiple_of(group * depth, depth), depth)], sem,
        )

    projected = jnp.dot(rows[0], weights[...], preferred_element_type=jnp.float32)
    cosines, sines = cosine[...], sine[...]

    def turned(head, gain):
        values = projected[:, head * dim : (head + 1) * dim]
        inverse = lax.rsqrt(jnp.mean(values * values, axis=-1, keepdims=True) + epsilon)
        scaled = values * gain
        return ((scaled * cosines + pltpu.roll(scaled, dim // 2, 1) * sines) * inverse).astype(
            jnp.bfloat16
        )

    for head in range(heads):
        query_out[head] = turned(head, gains[0:1, :])
    key_out[...] = turned(heads, gains[1:2, :])
    value_out[...] = projected[:, (heads + 1) * dim :].astype(jnp.bfloat16)


def project(meta, blocks, row_count, shards, cosine, sine, gains, heads):
    count, tile, width = blocks.shape
    keys = list(shards)
    depth, columns = shards[0, 0].shape
    dim = HEAD_DIMENSION
    places = width // depth // 2

    def spot(j, meta):
        return (meta[2 + j], 0)

    return pl.pallas_call(
        functools.partial(project_kernel, heads, places, keys),
        grid_spec=pltpu.PrefetchScalarGridSpec(
            num_scalar_prefetch=1,
            grid=(count,),
            in_specs=[
                pl.BlockSpec((1, tile, width), lambda j, meta: (j, 0, 0)),
                pl.BlockSpec((tile, dim), spot),
                pl.BlockSpec((tile, dim), spot),
                pl.BlockSpec((2, dim), lambda j, meta: (0, 0)),
            ]
            + [pl.BlockSpec(memory_space=pl.ANY)] * len(keys),
            out_specs=[
                pl.BlockSpec((heads, tile, dim), lambda j, meta: (0, meta[2 + j], 0)),
                pl.BlockSpec((tile, dim), spot),
                pl.BlockSpec((tile, dim), spot),
            ],
            scratch_shapes=[
                pltpu.VMEM((width, columns), jnp.bfloat16),
                pltpu.SemaphoreType.DMA,
            ],
        ),
        out_shape=[
            jax.ShapeDtypeStruct((heads, row_count, dim), jnp.bfloat16),
            jax.ShapeDtypeStruct((row_count, dim), jnp.bfloat16),
            jax.ShapeDtypeStruct((row_count, dim), jnp.bfloat16),
        ],
        compiler_params=pltpu.CompilerParams(vmem_limit_bytes=VMEM_LIMIT),
        cost_estimate=pl.CostEstimate(
            flops=2 * row_count * width * columns,
            bytes_accessed=2 * (row_count * width + width * columns + row_count * columns),
            transcendentals=0,
        ),
    )(meta, blocks, cosine, sine, gains, *[shards[key] for key in keys])


def attend_kernel(tile, meta, query, own_key, own_value, far_key, far_value, out, keys, values, total):
    heads, dim = query.shape[0], HEAD_DIMENSION
    row_count = own_key.shape[0]
    half = row_count // 2
    parity, length = meta[0], meta[1]
    step = pl.program_id(0)

    @pl.when(step == 0)
    def _():
        ones = jnp.ones((half, dim), jnp.bfloat16)
        for key_ref, value_ref, whose in ((own_key, own_value, parity), (far_key, far_value, 1 - parity)):
            for part in range(2):
                base = jnp.where(whose == 0, 3 * half * part, half * (1 + part))
                base = pl.multiple_of(base, half)
                source = pl.ds(part * half, half)
                keys[pl.ds(base, half), :] = key_ref[source, :]
                valid = base + lax.broadcasted_iota(jnp.int32, (half, dim), 0) < length
                zero = jnp.zeros((half, dim), jnp.bfloat16)
                values[pl.ds(base, half), :dim] = jnp.where(valid, value_ref[source, :], zero)
                values[pl.ds(base, half), dim:] = jnp.where(valid, ones, zero)

    first = step * tile
    first = first + jnp.where(parity == 0, jnp.where(first < half, 0, 2 * half), half)

    def weigh(head, start, width, masked):
        scores = lax.dot_general(
            query[head], keys[pl.ds(start, width), :], (((1,), (1,)), ((), ())),
            preferred_element_type=jnp.float32,
        )
        weights = jnp.exp2(scores)
        if masked:
            below = lax.broadcasted_iota(jnp.int32, weights.shape, 1) <= lax.broadcasted_iota(
                jnp.int32, weights.shape, 0
            )
            weights = jnp.where(below, weights, 0.0)
        return jnp.dot(
            weights.astype(jnp.bfloat16), values[pl.ds(start, width), :], preferred_element_type=jnp.float32
        )

    diagonal = pl.multiple_of(first, tile)
    for head in range(heads):
        total[head] = weigh(head, diagonal, tile, True)

    def wide(index, _):
        start = pl.multiple_of(index * half, half)
        for head in range(heads):
            total[head] += weigh(head, start, half, False)
        return 0

    lax.fori_loop(0, first // half, wide, 0)

    def narrow(index, _):
        start = pl.multiple_of(index * tile, tile)
        for head in range(heads):
            total[head] += weigh(head, start, tile, False)
        return 0

    lax.fori_loop(first // half * (half // tile), first // tile, narrow, 0)
    for head in range(heads):
        summed = total[head]
        out[:, head * dim : (head + 1) * dim] = (summed[:, :dim] / summed[:, dim:]).astype(jnp.bfloat16)


def attend(meta, query, own_key, own_value, far_key, far_value):
    heads, row_count, dim = query.shape
    tile = min(256, row_count // 2)
    whole = pl.BlockSpec((row_count, dim), lambda i, meta: (0, 0))
    return pl.pallas_call(
        functools.partial(attend_kernel, tile),
        grid_spec=pltpu.PrefetchScalarGridSpec(
            num_scalar_prefetch=1,
            grid=(row_count // tile,),
            in_specs=[pl.BlockSpec((heads, tile, dim), lambda i, meta: (0, i, 0))] + [whole] * 4,
            out_specs=pl.BlockSpec((tile, heads * dim), lambda i, meta: (i, 0)),
            scratch_shapes=[
                pltpu.VMEM((2 * row_count, dim), jnp.bfloat16),
                pltpu.VMEM((2 * row_count, 2 * dim), jnp.bfloat16),
                pltpu.VMEM((heads, tile, 2 * dim), jnp.float32),
            ],
        ),
        out_shape=jax.ShapeDtypeStruct((row_count, heads * dim), jnp.bfloat16),
        compiler_params=pltpu.CompilerParams(vmem_limit_bytes=VMEM_LIMIT),
        cost_estimate=pl.CostEstimate(
            flops=4 * heads * row_count * row_count * dim * 2,
            bytes_accessed=4 * heads * row_count * dim + 8 * row_count * dim,
            transcendentals=heads * row_count * row_count,
        ),
    )(meta, query, own_key, own_value, far_key, far_value)


def output_kernel(places, keys, meta, rows, *rest):
    shard_refs = rest[: len(keys)]
    out, weights, sem = rest[len(keys) :]
    columns = shard_refs[0].shape[1]

    @pl.when(pl.program_id(0) == 0)
    def _():
        load_shards(
            meta[0], meta[1], places, keys, shard_refs,
            lambda group: weights.at[:, pl.ds(pl.multiple_of(group * columns, columns), columns)], sem,
        )

    out[0] = jnp.dot(rows[...], weights[...], preferred_element_type=jnp.float32).astype(jnp.bfloat16)


def output_part(meta, attended, shards, blocks):
    row_count, depth = attended.shape
    keys = list(shards)
    columns = shards[0, 0].shape[1]
    places = (max(key[1] for key in keys)) + 1
    width = columns * 2 * places
    tile = row_count // blocks
    return pl.pallas_call(
        functools.partial(output_kernel, places, keys),
        grid_spec=pltpu.PrefetchScalarGridSpec(
            num_scalar_prefetch=1,
            grid=(blocks,),
            in_specs=[pl.BlockSpec((tile, depth), lambda j, meta: (meta[2 + j], 0))]
            + [pl.BlockSpec(memory_space=pl.ANY)] * len(keys),
            out_specs=pl.BlockSpec((1, tile, width), lambda j, meta: (j, 0, 0)),
            scratch_shapes=[pltpu.VMEM((depth, width), jnp.bfloat16), pltpu.SemaphoreType.DMA],
        ),
        out_shape=jax.ShapeDtypeStruct((blocks, tile, width), jnp.bfloat16),
        compiler_params=pltpu.CompilerParams(vmem_limit_bytes=VMEM_LIMIT),
        cost_estimate=pl.CostEstimate(
            flops=2 * row_count * width * depth,
            bytes_accessed=2 * (row_count * width + width * depth + row_count * depth),
            transcendentals=0,
        ),
    )(meta, attended, *[shards[key] for key in keys])


def per_device(
    hidden_in,
    norm_attention,
    norm_experts,
    query_master,
    trainer_key_value_weight,
    output_master,
    query_gain,
    key_gain,
    lengths,
    router,
    expert_gateup,
    expert_down,
    routes,
):
    experts_axis = lax.axis_size("expert")
    group_member = lax.axis_index("expert")
    group_index = lax.axis_index("group")
    heads = QUERY_HEADS // experts_axis
    dim = HEAD_DIMENSION
    rows_here, model_width = hidden_in.shape
    local_rows = rows_here * experts_axis

    common_head = group_member * heads // (QUERY_HEADS // KEY_VALUE_HEADS)
    pair = lax.dynamic_slice_in_dim(trainer_key_value_weight, common_head * dim, dim, 2)
    joined = jnp.concatenate([query_master, pair[0], pair[1]], axis=1).astype(jnp.bfloat16)
    joined_shards = gather_group(joined)
    blocks = gather_tokens(hidden_in)
    stages = 2 if output_master.shape[1] >= 256 else 1
    stage_width = output_master.shape[1] // stages
    output_shards = [
        gather_group(output_master[:, s * stage_width : (s + 1) * stage_width].astype(jnp.bfloat16))
        for s in range(stages)
    ]

    masks = doubling_masks(experts_axis)
    block_order = jnp.bitwise_xor(group_member, jnp.array(masks, jnp.int32))
    meta = jnp.concatenate([jnp.stack([group_index // 2, group_index % 2]), block_order]).astype(jnp.int32)

    parity = group_index % 2
    own_places = local_positions(parity, local_rows).astype(jnp.float32)
    exponents = jnp.arange(dim // 2).astype(jnp.float32)
    inverse = jnp.exp(exponents * (-2.0 * math.log(rope_theta) / dim))
    angles = own_places[:, None] * inverse[None, :]
    cosine_values, sine_values = jnp.cos(angles), jnp.sin(angles)
    cosine = jnp.concatenate([cosine_values, cosine_values], axis=1)
    sine = jnp.concatenate([-sine_values, sine_values], axis=1)
    gains = jnp.stack([query_gain * (dim**-0.5 * math.log2(math.e)), key_gain])
    normed = norm_rows(blocks, norm_attention).astype(jnp.bfloat16)
    query, key_rows, value_rows = project(
        meta, normed, local_rows, joined_shards, cosine, sine, gains, heads
    )

    partner = from_xor(jnp.stack([key_rows, value_rows]), "group", 1)
    valid_length = jnp.sum(jnp.where(jnp.arange(lengths.shape[0]) == group_index // 2, lengths, 0))
    attend_meta = jnp.stack([parity, valid_length]).astype(jnp.int32)
    attended = attend(attend_meta, query, key_rows, value_rows, partner[0], partner[1])

    sums = [
        scatter_sum(output_part(meta, attended, shards, experts_axis)) for shards in output_shards
    ]
    summed = jnp.stack([part.reshape(rows_here, -1, stage_width) for part in sums], axis=2).reshape(
        rows_here, model_width
    )
    hidden = (hidden_in.astype(jnp.float32) + summed).astype(jnp.bfloat16)

    normed_second = norm_rows(hidden, norm_experts).astype(jnp.bfloat16)
    logits = jnp.dot(normed_second, router, preferred_element_type=jnp.float32)
    route_table = routes[:, :, None] == jnp.arange(logits.shape[1])[None, None, :]
    picked = jnp.sum(jnp.where(route_table, logits[:, None, :], 0.0), axis=-1)
    raised = jnp.exp(picked)
    gate_values = raised / jnp.sum(raised, axis=1, keepdims=True)
    inside = routes < experts_axis
    gate_window = jnp.sum(jnp.where(inside, gate_values, 0.0), axis=1)
    expert_window = jnp.sum(jnp.where(inside, routes, 0), axis=1)
    present = jnp.any(inside, axis=1)
    capacity = local_rows // (experts_axis * experts_axis)
    member_table = (
        present[:, None] & (expert_window[:, None] == jnp.arange(experts_axis)[None, :])
    ).astype(jnp.int32)
    ranking = jnp.sum(jnp.cumsum(member_table, axis=0) * member_table, axis=1) - 1
    slot_index = expert_window * capacity + ranking
    select = (
        (jnp.arange(experts_axis * capacity)[:, None] == slot_index[None, :]) & present[None, :]
    ).astype(jnp.bfloat16)
    outgoing = (
        jnp.dot(select, normed_second, preferred_element_type=jnp.float32)
        .astype(jnp.bfloat16)
        .reshape(experts_axis, capacity, model_width)
    )
    gateup_here = expert_gateup[0]
    down_here = expert_down[0]
    hidden_units = down_here.shape[0]
    slot_items = lax.all_to_all(outgoing, "expert", split_axis=0, concat_axis=0, tiled=True)
    flattened = slot_items.reshape(-1, slot_items.shape[-1])
    gate_up = jnp.dot(flattened, gateup_here, preferred_element_type=jnp.float32)
    active = (jax.nn.silu(gate_up[:, :hidden_units]) * gate_up[:, hidden_units:]).astype(
        jnp.bfloat16
    )
    result = (
        jnp.dot(active, down_here, preferred_element_type=jnp.float32)
        .astype(jnp.bfloat16)
        .reshape(slot_items.shape)
    )
    returned = lax.all_to_all(result, "expert", split_axis=0, concat_axis=0, tiled=True)
    combined = jnp.dot(
        jnp.transpose(select), returned.reshape(-1, model_width), preferred_element_type=jnp.float32
    )
    expert_mix = (gate_window[:, None] * combined).astype(jnp.bfloat16)
    return (hidden, expert_mix)


def solution(mesh):
    return jax.shard_map(
        per_device,
        mesh=mesh,
        in_specs=(
            P(("group", "expert"), None),
            P(),
            P(),
            P("group", "expert"),
            P(None, "group", None),
            P("expert", "group"),
            P(),
            P(),
            P(),
            P(),
            P("expert", None, None),
            P("expert", None, None),
            P(("group", "expert"), None),
        ),
        out_specs=(P(("group", "expert"), None), P(("group", "expert"), None)),
        check_vma=False,
    )
```

```python
import functools
import math

import jax
import jax.numpy as jnp
from jax import lax
from jax.experimental import pallas as pl
from jax.experimental.pallas import tpu as pltpu
from jax.sharding import PartitionSpec as P

QUERY_HEADS = 32
KEY_VALUE_HEADS = 4
HEAD_DIMENSION = 128

epsilon = 1e-06
rope_theta = 1000000.0
VMEM_LIMIT = 56 * 1024 * 1024
STAGE_WIDTH = 128
FREE = pl.CostEstimate(flops=0, bytes_accessed=0, transcendentals=0)


def norm_rows(values, gain_vector):
    widened = values.astype(jnp.float32)
    inverse_rms = lax.rsqrt(jnp.mean(widened * widened, axis=-1, keepdims=True) + epsilon)
    return widened * inverse_rms * gain_vector


def local_positions(parity, row_count):
    indices = jnp.arange(row_count)
    quarter = row_count // 2
    offset = jnp.where(parity == 0, jnp.where(indices < quarter, 0, 2 * quarter), quarter)
    return indices + offset


def from_xor(block, axis, mask):
    count = lax.axis_size(axis)
    return lax.ppermute(block, axis, [(i, i ^ mask) for i in range(count)])


def cross(block):
    return from_xor(block, "group", 1)


def after(block, *others):
    return lax.optimization_barrier((block, *others))[0]


LINE = ((0, 1, 2, 3), (1, 0, 2, 3), (2, 3, 1, 0), (3, 2, 1, 0))
PAIRS = ((0, 1), (1, 0), (2, 3), (3, 2))
MIDDLE = ((1, 2), (2, 1))
OUTWARD = ((1, 0), (2, 3))


def along(block, moves):
    return lax.ppermute(block, "group", [(2 * a + s, 2 * b + s) for a, b in moves for s in range(2)])


def line_rounds(block):
    place = lax.axis_index("group") // 2
    edge = (place == 0) | (place == 3)
    crossed = [None] * 4
    crossed[0], near, inner = yield cross(block), along(block, PAIRS), along(block, MIDDLE)
    crossed[1], inner_far, outer = yield cross(near), along(near, MIDDLE), along(inner, OUTWARD)
    third = jnp.where(edge, outer, inner)
    crossed[2], outer = yield cross(third), along(inner_far, OUTWARD)
    fourth = jnp.where(edge, outer, inner_far)
    (crossed[3],) = yield (cross(fourth),)
    return [block, near, third, fourth] + crossed


def advance(rounds, results=None):
    try:
        return lax.optimization_barrier(rounds.send(results)), None
    except StopIteration as end:
        return None, end.value


def gather_chain(block, start=(), ready=()):
    if lax.axis_size("group") != 8:
        return [(block,)] * 4, list(lax.all_gather(block, "group"))
    chain = line_rounds(after(block, *start))
    brought = [None]
    for step in range(4):
        if step == 3 and ready:
            brought[-1] = after(brought[-1], *ready)
        brought.append(advance(chain, brought[-1])[0])
    return brought[1:], advance(chain, brought[-1])[1]


def held_groups(place, side):
    groups = lax.axis_size("group")
    if groups != 8:
        return jnp.arange(groups)
    places = jnp.sum(jnp.where(jnp.arange(4)[:, None] == place, jnp.array(LINE, jnp.int32), 0), axis=0)
    return jnp.concatenate([2 * places + side, 2 * places + 1 - side])


def doubling_masks(count):
    masks, stride = [0], count // 2
    while stride:
        masks = masks + [mask ^ stride for mask in masks]
        stride //= 2
    return masks


def gather_tokens(rows):
    blocks = [rows]
    stride = lax.axis_size("expert") // 2
    while stride:
        blocks = blocks + [from_xor(block, "expert", stride) for block in blocks]
        stride //= 2
    return blocks


def scatter_sum(kept, sent):
    stride = 1
    while True:
        half = kept.shape[0] // 2
        arrived = from_xor(sent, "expert", stride)
        if not half:
            return kept[0], arrived[0]
        summed = [
            kept[part].astype(jnp.float32) + arrived[part].astype(jnp.float32)
            for part in (slice(None, half), slice(half, None))
        ]
        kept, sent = [part.astype(jnp.bfloat16) for part in summed]
        stride *= 2


def stack_shards(meta, shard_refs, weights):
    depth = weights.shape[0] // len(shard_refs)
    for index, ref in enumerate(shard_refs):
        weights[pl.ds(pl.multiple_of(meta[index] * depth, depth), depth), :] = ref[...]


def turn(values, cosines, sines, mixer):
    values = values.astype(jnp.bfloat16)
    wide = values.astype(jnp.float32)
    both = jnp.concatenate([values, (wide * wide).astype(jnp.bfloat16)], axis=1)
    mixed = jnp.dot(both, mixer, preferred_element_type=jnp.float32)
    dim = values.shape[1]
    inverse = lax.rsqrt(mixed[:, dim:] + epsilon)
    return ((wide * cosines + mixed[:, :dim] * sines) * inverse).astype(jnp.bfloat16)


def query_kernel(shard_count, meta, rows, cosine, sine, mixer, *rest):
    count, tile, width = rows.shape
    dim = HEAD_DIMENSION
    if shard_count > 1:
        query_out, weights = rest[shard_count:]
        stack_shards(meta, rest[:shard_count], weights)
        columns = weights[...]
    else:
        query_out = rest[1]
        columns = rest[0][...].reshape(width, 2 * dim)
    projected = jnp.dot(rows[...].reshape(count * tile, width), columns, preferred_element_type=jnp.float32)
    for block in range(count):
        spot = pl.ds(pl.multiple_of(meta[meta.shape[0] - count + block] * tile, tile), tile)
        here = slice(block * tile, (block + 1) * tile)
        for head in range(2):
            query_out[head, here, :] = turn(
                projected[here, head * dim : (head + 1) * dim], cosine[spot, :], sine[spot, :], mixer[...]
            )


def key_kernel(shard_count, meta, rows, cosine, sine, mixer, *rest):
    pair_out, weights = rest[shard_count:]
    stack_shards(meta, rest[:shard_count], weights)
    count, tile, width = rows.shape
    dim = HEAD_DIMENSION
    projected = jnp.dot(
        rows[...].reshape(count * tile, width), weights[...], preferred_element_type=jnp.float32
    )
    for block in range(count):
        spot = pl.ds(pl.multiple_of(meta[shard_count + block] * tile, tile), tile)
        here = slice(block * tile, (block + 1) * tile)
        pair_out[0, spot, :] = turn(projected[here, :dim], cosine[spot, :], sine[spot, :], mixer[...])
        pair_out[1, spot, :] = projected[here, dim:].astype(jnp.bfloat16)


def project(kernel, first, steps, meta, blocks, shards, cosine, sine, mixer):
    count, tile, width = blocks.shape
    dim = HEAD_DIMENSION
    shard_count = len(shards)
    if shard_count > 1:
        shard = pl.BlockSpec((shards[0].shape[0], 2 * dim), lambda n, meta: (0, first + n))
        scratch = [pltpu.VMEM((width, 2 * dim), jnp.bfloat16)]
    else:
        shard = pl.BlockSpec((*shards[0].shape[:2], 2 * dim), lambda n, meta: (0, 0, first + n))
        scratch = []
    table = pl.BlockSpec((count * tile, dim), lambda n, meta: (0, 0))
    return pl.pallas_call(
        functools.partial(kernel, shard_count),
        grid_spec=pltpu.PrefetchScalarGridSpec(
            num_scalar_prefetch=1,
            grid=(steps,),
            in_specs=[
                pl.BlockSpec((count, tile, width), lambda n, meta: (0, 0, 0)),
                table,
                table,
                pl.BlockSpec((2 * dim, 2 * dim), lambda n, meta: (0, 0)),
            ]
            + [shard] * shard_count,
            out_specs=pl.BlockSpec((2, count * tile, dim), lambda n, meta: (n, 0, 0)),
            scratch_shapes=scratch,
        ),
        out_shape=jax.ShapeDtypeStruct((2 * steps, count * tile, dim), jnp.bfloat16),
        compiler_params=pltpu.CompilerParams(vmem_limit_bytes=VMEM_LIMIT),
        cost_estimate=pl.CostEstimate(
            flops=4 * steps * count * tile * width * dim,
            bytes_accessed=2 * (count * tile * width + steps * 2 * dim * (width + count * tile)),
            transcendentals=0,
        ),
    )(meta, blocks, cosine, sine, mixer, *shards)


def attend_kernel(tile, meta, own, far, *rest):
    *queries, out, keys, values, total = rest
    heads, dim = total.shape[0], HEAD_DIMENSION
    query = [part.at[head] for part in queries for head in range(part.shape[0])]
    row_count = own.shape[1]
    half = row_count // 2
    parity, length = meta[0], meta[1]
    step = pl.program_id(0)

    @pl.when(step == 0)
    def _():
        ones = jnp.ones((half, dim), jnp.bfloat16)
        for pair, whose in ((own, parity), (far, 1 - parity)):
            for part in range(2):
                base = jnp.where(whose == 0, 3 * half * part, half * (1 + part))
                base = pl.multiple_of(base, half)
                source = pl.ds(part * half, half)
                keys[pl.ds(base, half), :] = pair[0, source, :]
                valid = base + lax.broadcasted_iota(jnp.int32, (half, dim), 0) < length
                zero = jnp.zeros((half, dim), jnp.bfloat16)
                values[pl.ds(base, half), :dim] = jnp.where(valid, pair[1, source, :], zero)
                values[pl.ds(base, half), dim:] = jnp.where(valid, ones, zero)

    first = meta[2 + step] * tile
    first = first + jnp.where(parity == 0, jnp.where(first < half, 0, 2 * half), half)

    def weigh(head, start, width, masked):
        scores = lax.dot_general(
            query[head][...], keys[pl.ds(start, width), :], (((1,), (1,)), ((), ())),
            preferred_element_type=jnp.float32,
        )
        weights = jnp.exp2(scores)
        if masked:
            below = lax.broadcasted_iota(jnp.int32, weights.shape, 1) <= lax.broadcasted_iota(
                jnp.int32, weights.shape, 0
            )
            weights = jnp.where(below, weights, 0.0)
        return jnp.dot(
            weights.astype(jnp.bfloat16), values[pl.ds(start, width), :], preferred_element_type=jnp.float32
        )

    diagonal = pl.multiple_of(first, tile)
    for head in range(heads):
        total[head] = weigh(head, diagonal, tile, True)

    def wide(index, _):
        start = pl.multiple_of(index * half, half)
        for head in range(heads):
            total[head] += weigh(head, start, half, False)
        return 0

    lax.fori_loop(0, first // half, wide, 0)

    def narrow(index, _):
        start = pl.multiple_of(index * tile, tile)
        for head in range(heads):
            total[head] += weigh(head, start, tile, False)
        return 0

    lax.fori_loop(first // half * (half // tile), first // tile, narrow, 0)
    for head in range(heads):
        summed = total[head]
        out[:, head * dim : (head + 1) * dim] = (summed[:, :dim] / summed[:, dim:]).astype(jnp.bfloat16)


def attend(meta, queries, own, far, tile):
    _, row_count, dim = queries[0].shape
    heads = sum(part.shape[0] for part in queries)
    whole = pl.BlockSpec((2, row_count, dim), lambda i, meta: (0, 0, 0))
    return pl.pallas_call(
        functools.partial(attend_kernel, tile),
        grid_spec=pltpu.PrefetchScalarGridSpec(
            num_scalar_prefetch=1,
            grid=(row_count // tile,),
            in_specs=[whole] * 2
            + [pl.BlockSpec((part.shape[0], tile, dim), lambda i, meta: (0, i, 0)) for part in queries],
            out_specs=pl.BlockSpec((tile, heads * dim), lambda i, meta: (i, 0)),
            scratch_shapes=[
                pltpu.VMEM((2 * row_count, dim), jnp.bfloat16),
                pltpu.VMEM((2 * row_count, 2 * dim), jnp.bfloat16),
                pltpu.VMEM((heads, tile, 2 * dim), jnp.float32),
            ],
        ),
        out_shape=jax.ShapeDtypeStruct((row_count, heads * dim), jnp.bfloat16),
        compiler_params=pltpu.CompilerParams(vmem_limit_bytes=VMEM_LIMIT),
        cost_estimate=FREE,
    )(meta, own, far, *queries)


def output_kernel(shard_count, meta, rows, *rest):
    kept, sent, weights = rest[shard_count:]
    width = STAGE_WIDTH
    if shard_count > 1:
        shards = [ref[...] for ref in rest[:shard_count]]
    else:
        shards = [rest[0][group] for group in range(rest[0].shape[0])]
    for index, shard in enumerate(shards):
        weights[:, pl.ds(pl.multiple_of(meta[index] * width, width), width)] = shard
    half = rows.shape[0] // 2
    for part, out in enumerate((kept, sent)):
        left = rows[part * half : (part + 1) * half].reshape(-1, rows.shape[2])
        product = jnp.dot(left, weights[...], preferred_element_type=jnp.float32)
        out[...] = product.astype(jnp.bfloat16).reshape(out.shape)


def output_part(meta, rows, shards, groups):
    count, tile, depth = rows.shape
    half, width = count // 2, groups * STAGE_WIDTH

    def whole(shape):
        return pl.BlockSpec(shape, lambda n, meta: (0,) * len(shape))

    return pl.pallas_call(
        functools.partial(output_kernel, len(shards)),
        grid_spec=pltpu.PrefetchScalarGridSpec(
            num_scalar_prefetch=1,
            grid=(1,),
            in_specs=[whole(rows.shape)] + [whole(shard.shape) for shard in shards],
            out_specs=[whole((half, tile, width))] * 2,
            scratch_shapes=[pltpu.VMEM((depth, width), jnp.bfloat16)],
        ),
        out_shape=[jax.ShapeDtypeStruct((half, tile, width), jnp.bfloat16)] * 2,
        compiler_params=pltpu.CompilerParams(vmem_limit_bytes=VMEM_LIMIT),
        cost_estimate=FREE,
    )(meta, rows, *shards)


def finish_kernel(states, gain, *rest):
    *terms, hidden_out, normed_out = rest
    stages = len(terms) // 2
    width = STAGE_WIDTH
    for stage in range(stages):
        total = terms[2 * stage][...].astype(jnp.float32) + terms[2 * stage + 1][...].astype(jnp.float32)
        for group in range(total.shape[1] // width):
            start = (group * stages + stage) * width
            here = slice(start, start + width)
            value = states[:, here].astype(jnp.float32) + total[:, group * width : (group + 1) * width]
            hidden_out[:, here] = value.astype(jnp.bfloat16)
    hidden = hidden_out[...].astype(jnp.float32)
    inverse = lax.rsqrt(jnp.mean(hidden * hidden, axis=-1, keepdims=True) + epsilon)
    normed_out[...] = (hidden * inverse * gain[...]).astype(jnp.bfloat16)


def finish(states, gain, terms):
    rows, width = states.shape
    tile = min(64, rows)

    def block(columns):
        return pl.BlockSpec((tile, columns), lambda i: (i, 0))

    return pl.pallas_call(
        finish_kernel,
        grid=(rows // tile,),
        in_specs=[block(width), pl.BlockSpec((1, width), lambda i: (0, 0))]
        + [block(term.shape[1]) for term in terms],
        out_specs=[block(width)] * 2,
        out_shape=[jax.ShapeDtypeStruct((rows, width), jnp.bfloat16)] * 2,
        compiler_params=pltpu.CompilerParams(vmem_limit_bytes=VMEM_LIMIT),
        cost_estimate=FREE,
    )(states, gain[None, :], *terms)


def per_device(
    hidden_in,
    norm_attention,
    norm_experts,
    query_master,
    trainer_key_value_weight,
    output_master,
    query_gain,
    key_gain,
    lengths,
    router,
    expert_gateup,
    expert_down,
    routes,
):
    experts_axis = lax.axis_size("expert")
    group_member = lax.axis_index("expert")
    group_index = lax.axis_index("group")
    heads = QUERY_HEADS // experts_axis
    dim = HEAD_DIMENSION
    rows_here, model_width = hidden_in.shape
    local_rows = rows_here * experts_axis

    groups = lax.axis_size("group")
    place, side = group_index // 2, group_index % 2
    common_head = group_member * heads // (QUERY_HEADS // KEY_VALUE_HEADS)
    pair = lax.dynamic_slice_in_dim(trainer_key_value_weight, common_head * dim, dim, 2)
    joined = jnp.concatenate([pair[0], pair[1]], axis=1).astype(jnp.bfloat16)
    query_all = lax.all_gather(query_master.astype(jnp.bfloat16), "group")
    stages = output_master.shape[1] // STAGE_WIDTH
    output_here = [
        output_master[:, stage * STAGE_WIDTH : (stage + 1) * STAGE_WIDTH].astype(jnp.bfloat16)
        for stage in range(stages)
    ]
    blocks = gather_tokens(after(hidden_in, joined))
    normed = jnp.stack([norm_rows(block, norm_attention).astype(jnp.bfloat16) for block in blocks])
    pair_rounds, pair_shards = gather_chain(joined)

    masks = doubling_masks(experts_axis)
    block_order = jnp.bitwise_xor(group_member, jnp.array(masks, jnp.int32))
    held = held_groups(place, side)
    meta = jnp.concatenate([held, block_order]).astype(jnp.int32)

    parity = side
    own_places = local_positions(parity, local_rows).astype(jnp.float32)
    exponents = jnp.arange(dim // 2).astype(jnp.float32)
    inverse = jnp.exp(exponents * (-2.0 * math.log(rope_theta) / dim))
    angles = own_places[:, None] * inverse[None, :]
    cosine_values, sine_values = jnp.cos(angles), jnp.sin(angles)
    cosine = jnp.concatenate([cosine_values, cosine_values], axis=1)
    sine = jnp.concatenate([-sine_values, sine_values], axis=1)

    def tables(gain):
        return cosine * gain, sine * jnp.roll(gain, dim // 2)

    lanes = jnp.arange(dim)
    swap = (lanes[:, None] == (lanes[None, :] + dim // 2) % dim).astype(jnp.float32)
    nothing = jnp.zeros((dim, dim), jnp.float32)
    mixer = jnp.block([[swap, nothing], [nothing, nothing + 1.0 / dim]]).astype(jnp.bfloat16)
    query_tables = tables(query_gain * (dim**-0.5 * math.log2(math.e)))
    key_tables = tables(key_gain)
    own_pair = project(key_kernel, 0, 1, meta, normed, pair_shards, *key_tables, mixer)
    far_pair = cross(own_pair)
    _, output_shards = gather_chain(output_here[0], pair_rounds[-1], (far_pair,))
    stage_shards = [output_shards] + [[lax.all_gather(part, "group")] for part in output_here[1:]]
    queries = [project(query_kernel, 0, heads // 2, meta, normed, [query_all], *query_tables, mixer)]

    valid_length = jnp.sum(jnp.where(jnp.arange(lengths.shape[0]) == group_index // 2, lengths, 0))
    attend_meta = jnp.concatenate([jnp.stack([parity, valid_length]), block_order]).astype(jnp.int32)
    attended = attend(attend_meta, queries, own_pair, far_pair, rows_here)

    attended = attended.reshape(experts_axis, rows_here, heads * dim)
    terms = []
    for stage, shards in enumerate(stage_shards):
        order = held if len(shards) > 1 else jnp.arange(groups)
        terms += scatter_sum(*output_part(order.astype(jnp.int32), attended, shards, groups))
    hidden, normed_second = finish(hidden_in, norm_experts, terms)

    logits = jnp.dot(normed_second, router, preferred_element_type=jnp.float32)
    route_table = routes[:, :, None] == jnp.arange(logits.shape[1])[None, None, :]
    picked = jnp.sum(jnp.where(route_table, logits[:, None, :], 0.0), axis=-1)
    raised = jnp.exp(picked)
    gate_values = raised / jnp.sum(raised, axis=1, keepdims=True)
    inside = routes < experts_axis
    gate_window = jnp.sum(jnp.where(inside, gate_values, 0.0), axis=1)
    expert_window = jnp.sum(jnp.where(inside, routes, 0), axis=1)
    present = jnp.any(inside, axis=1)
    capacity = local_rows // (experts_axis * experts_axis)
    member_table = (present[:, None] & (expert_window[:, None] == block_order[None, :])).astype(jnp.int32)
    ranking = jnp.cumsum(member_table, axis=0) - 1
    slot_index = jnp.sum(member_table * (ranking + jnp.arange(experts_axis) * capacity), axis=1)
    select = (
        (jnp.arange(experts_axis * capacity)[:, None] == slot_index[None, :]) & present[None, :]
    ).astype(jnp.bfloat16)
    outgoing = (
        jnp.dot(select, normed_second, preferred_element_type=jnp.float32)
        .astype(jnp.bfloat16)
        .reshape(experts_axis, capacity, model_width)
    )

    def exchange(slots):
        return jnp.stack([slots[0]] + [from_xor(slots[j], "expert", masks[j]) for j in range(1, experts_axis)])

    gateup_here = expert_gateup[0]
    down_here = expert_down[0]
    hidden_units = down_here.shape[0]
    slot_items = exchange(outgoing)
    flattened = slot_items.reshape(-1, slot_items.shape[-1])
    gate_up = jnp.dot(flattened, gateup_here, preferred_element_type=jnp.float32)
    active = (jax.nn.silu(gate_up[:, :hidden_units]) * gate_up[:, hidden_units:]).astype(
        jnp.bfloat16
    )
    result = (
        jnp.dot(active, down_here, preferred_element_type=jnp.float32)
        .astype(jnp.bfloat16)
        .reshape(slot_items.shape)
    )
    returned = exchange(result)
    combined = jnp.dot(
        jnp.transpose(select), returned.reshape(-1, model_width), preferred_element_type=jnp.float32
    )
    expert_mix = (gate_window[:, None] * combined).astype(jnp.bfloat16)
    return (hidden, expert_mix)


def solution(mesh):
    return jax.shard_map(
        per_device,
        mesh=mesh,
        in_specs=(
            P(("group", "expert"), None),
            P(),
            P(),
            P("group", "expert"),
            P(None, "group", None),
            P("expert", "group"),
            P(),
            P(),
            P(),
            P(),
            P("expert", None, None),
            P("expert", None, None),
            P(("group", "expert"), None),
        ),
        out_specs=(P(("group", "expert"), None), P(("group", "expert"), None)),
        check_vma=False,
    )
```

```python
import functools
import math

import jax
import jax.numpy as jnp
from jax import lax
from jax.experimental import pallas as pl
from jax.experimental.pallas import tpu as pltpu
from jax.sharding import PartitionSpec as P

QUERY_HEADS = 32
KEY_VALUE_HEADS = 4
HEAD_DIMENSION = 128

epsilon = 1e-06
rope_theta = 1000000.0
VMEM_LIMIT = 32 * 1024 * 1024
FREE = pl.CostEstimate(flops=0, bytes_accessed=0, transcendentals=0)


def norm_rows(values, gain_vector):
    widened = values.astype(jnp.float32)
    inverse_rms = lax.rsqrt(jnp.mean(widened * widened, axis=-1, keepdims=True) + epsilon)
    return widened * inverse_rms * gain_vector


def local_positions(parity, row_count):
    indices = jnp.arange(row_count)
    quarter = row_count // 2
    offset = jnp.where(parity == 0, jnp.where(indices < quarter, 0, 2 * quarter), quarter)
    return indices + offset


def from_xor(block, axis, mask):
    count = lax.axis_size(axis)
    return lax.ppermute(block, axis, [(i, i ^ mask) for i in range(count)])


def cross(block):
    return from_xor(block, "group", 1)


def after(block, *others):
    return lax.optimization_barrier((block, *others))[0]


LINE = ((0, 1, 2, 3), (1, 0, 2, 3), (2, 3, 1, 0), (3, 2, 1, 0))
PAIRS = ((0, 1), (1, 0), (2, 3), (3, 2))
MIDDLE = ((1, 2), (2, 1))
OUTWARD = ((1, 0), (2, 3))


def along(block, moves):
    return lax.ppermute(block, "group", [(2 * a + s, 2 * b + s) for a, b in moves for s in range(2)])


def line_rounds(block, shards, crossed):
    place = lax.axis_index("group") // 2
    edge = (place == 0) | (place == 3)
    shards[0] = block
    if crossed is None:
        shards[1], inner, shards[4] = yield along(block, PAIRS), along(block, MIDDLE), cross(block)
    else:
        shards[4] = crossed
        shards[1], inner = yield along(block, PAIRS), along(block, MIDDLE)
    shards[5], inner_far, outer = yield cross(shards[1]), along(shards[1], MIDDLE), along(inner, OUTWARD)
    shards[2] = jnp.where(edge, outer, inner)
    shards[6], outer = yield cross(shards[2]), along(inner_far, OUTWARD)
    shards[3] = jnp.where(edge, outer, inner_far)
    (shards[7],) = yield (cross(shards[3]),)
    yield ()


class Beside:
    def __init__(self, block, crossed=None):
        groups = lax.axis_size("group")
        self.found = [None] * groups if groups == 8 else list(lax.all_gather(block, "group"))
        self.chain = line_rounds(block, self.found, crossed) if groups == 8 else None
        self.brought = (block,) if self.chain is None else lax.optimization_barrier(next(self.chain))

    def round(self, *ready):
        if self.chain is not None:
            results = after(self.brought, *ready)
            self.brought = lax.optimization_barrier(self.chain.send(results))

    def token(self):
        return self.brought[0]

    def held(self, indices):
        if self.chain is not None and any(self.found[index] is None for index in indices):
            self.chain.send(self.brought)
            self.chain = None
        return [self.found[index] for index in indices]


def held_groups(place, side):
    groups = lax.axis_size("group")
    if groups != 8:
        return jnp.arange(groups)
    places = jnp.sum(jnp.where(jnp.arange(4)[:, None] == place, jnp.array(LINE, jnp.int32), 0), axis=0)
    return jnp.concatenate([2 * places + side, 2 * places + 1 - side])


def doubling_masks(count):
    masks, stride = [0], count // 2
    while stride:
        masks = masks + [mask ^ stride for mask in masks]
        stride //= 2
    return masks


def gather_tokens(rows):
    blocks = [rows]
    stride = lax.axis_size("expert") // 2
    while stride:
        blocks = blocks + [from_xor(block, "expert", stride) for block in blocks]
        stride //= 2
    return blocks


def scatter_sum(kept, sent):
    stride = 1
    while True:
        half = kept.shape[0] // 2
        arrived = from_xor(sent, "expert", stride)
        if not half:
            return (kept[0], arrived[0]), sent
        summed = [
            kept[part].astype(jnp.float32) + arrived[part].astype(jnp.float32)
            for part in (slice(None, half), slice(half, None))
        ]
        kept, sent = [part.astype(jnp.bfloat16) for part in summed]
        stride *= 2


def stack_shards(meta, refs, weights):
    depth = weights.shape[0] // len(refs)
    for index, ref in enumerate(refs):
        weights[pl.ds(pl.multiple_of(meta[2 + index] * depth, depth), depth), :] = ref[...]


def turn(values, cosines, sines, mixer):
    values = values.astype(jnp.bfloat16)
    wide = values.astype(jnp.float32)
    both = jnp.concatenate([values, (wide * wide).astype(jnp.bfloat16)], axis=1)
    mixed = jnp.dot(both, mixer, preferred_element_type=jnp.float32)
    dim = values.shape[1]
    inverse = lax.rsqrt(mixed[:, dim:] + epsilon)
    return ((wide * cosines + mixed[:, :dim] * sines) * inverse).astype(jnp.bfloat16)


def query_kernel(count, meta, *rest):
    rows, (cosine, sine, mixer, *rest) = rest[:count], rest[count:]
    *shards, query_out, weights = rest
    stack_shards(meta, shards, weights)
    tile, dim = rows[0].shape[0], HEAD_DIMENSION
    joined = jnp.concatenate([block[...] for block in rows], axis=0)
    projected = jnp.dot(joined, weights[...], preferred_element_type=jnp.float32)
    for block in range(count):
        spot = pl.ds(pl.multiple_of(meta[2 + len(shards) + block] * tile, tile), tile)
        here = slice(block * tile, (block + 1) * tile)
        for head in range(2):
            query_out[head, here, :] = turn(
                projected[here, head * dim : (head + 1) * dim], cosine[spot, :], sine[spot, :], mixer[...]
            )


def key_kernel(count, meta, *rest):
    rows, (cosine, sine, mixer, *rest) = rest[:count], rest[count:]
    *shards, pair_out, weights = rest
    stack_shards(meta, shards, weights)
    tile, dim = rows[0].shape[0], HEAD_DIMENSION
    joined = jnp.concatenate([block[...] for block in rows], axis=0)
    projected = jnp.dot(joined, weights[...], preferred_element_type=jnp.float32)
    for block in range(count):
        spot = pl.ds(pl.multiple_of(meta[2 + len(shards) + block] * tile, tile), tile)
        here = slice(block * tile, (block + 1) * tile)
        pair_out[0, spot, :] = turn(projected[here, :dim], cosine[spot, :], sine[spot, :], mixer[...])
        pair_out[1, spot, :] = projected[here, dim:].astype(jnp.bfloat16)


def project(kernel, first, steps, meta, blocks, shards, cosine, sine, mixer):
    count, (tile, width) = len(blocks), blocks[0].shape
    dim = HEAD_DIMENSION
    shard = pl.BlockSpec((shards[0].shape[0], 2 * dim), lambda n, meta: (0, first + n))
    table = pl.BlockSpec((count * tile, dim), lambda n, meta: (0, 0))
    return pl.pallas_call(
        functools.partial(kernel, count),
        grid_spec=pltpu.PrefetchScalarGridSpec(
            num_scalar_prefetch=1,
            grid=(steps,),
            in_specs=[pl.BlockSpec((tile, width), lambda n, meta: (0, 0))] * count
            + [
                table,
                table,
                pl.BlockSpec((2 * dim, 2 * dim), lambda n, meta: (0, 0)),
            ]
            + [shard] * len(shards),
            out_specs=pl.BlockSpec((2, count * tile, dim), lambda n, meta: (n, 0, 0)),
            scratch_shapes=[pltpu.VMEM((width, 2 * dim), jnp.bfloat16)],
        ),
        out_shape=jax.ShapeDtypeStruct((2 * steps, count * tile, dim), jnp.bfloat16),
        compiler_params=pltpu.CompilerParams(vmem_limit_bytes=VMEM_LIMIT),
        cost_estimate=pl.CostEstimate(
            flops=16 * steps * count * tile * width * dim, bytes_accessed=2 * count * tile * width, transcendentals=0
        ),
    )(meta, *blocks, cosine, sine, mixer, *shards)


def attend_kernel(tile, start, meta, own, far, *rest):
    *queries, out, keys, values, total = rest
    heads, dim = total.shape[0], HEAD_DIMENSION
    query = [part.at[head] for part in queries for head in range(part.shape[0])]
    row_count = own.shape[1]
    half = row_count // 2
    parity, length = meta[0], meta[1]
    step = pl.program_id(0)

    @pl.when(step == 0)
    def _():
        ones = jnp.ones((half, dim), jnp.bfloat16)
        for pair, whose in ((own, parity), (far, 1 - parity)):
            for part in range(2):
                base = jnp.where(whose == 0, 3 * half * part, half * (1 + part))
                base = pl.multiple_of(base, half)
                source = pl.ds(part * half, half)
                keys[pl.ds(base, half), :] = pair[0, source, :]
                valid = base + lax.broadcasted_iota(jnp.int32, (half, dim), 0) < length
                zero = jnp.zeros((half, dim), jnp.bfloat16)
                values[pl.ds(base, half), :dim] = jnp.where(valid, pair[1, source, :], zero)
                values[pl.ds(base, half), dim:] = jnp.where(valid, ones, zero)

    first = meta[2 + start + step] * tile
    first = first + jnp.where(parity == 0, jnp.where(first < half, 0, 2 * half), half)

    def weigh(head, start, width, masked):
        scores = lax.dot_general(
            query[head][...], keys[pl.ds(start, width), :], (((1,), (1,)), ((), ())),
            preferred_element_type=jnp.float32,
        )
        weights = jnp.exp2(scores)
        if masked:
            below = lax.broadcasted_iota(jnp.int32, weights.shape, 1) <= lax.broadcasted_iota(
                jnp.int32, weights.shape, 0
            )
            weights = jnp.where(below, weights, 0.0)
        return jnp.dot(
            weights.astype(jnp.bfloat16), values[pl.ds(start, width), :], preferred_element_type=jnp.float32
        )

    diagonal = pl.multiple_of(first, tile)
    for head in range(heads):
        total[head] = weigh(head, diagonal, tile, True)

    def wide(index, _):
        start = pl.multiple_of(index * half, half)
        for head in range(heads):
            total[head] += weigh(head, start, half, False)
        return 0

    lax.fori_loop(0, first // half, wide, 0)

    def narrow(index, _):
        start = pl.multiple_of(index * tile, tile)
        for head in range(heads):
            total[head] += weigh(head, start, tile, False)
        return 0

    lax.fori_loop(first // half * (half // tile), first // tile, narrow, 0)
    for head in range(heads):
        summed = total[head]
        out[:, head * dim : (head + 1) * dim] = (summed[:, :dim] / summed[:, dim:]).astype(jnp.bfloat16)


def attend(meta, queries, own, far, tile, part):
    _, row_count, dim = queries[0].shape
    heads = sum(query.shape[0] for query in queries)
    steps = row_count // tile // 2
    start = part * steps
    whole = pl.BlockSpec((2, row_count, dim), lambda i, meta: (0, 0, 0))
    return pl.pallas_call(
        functools.partial(attend_kernel, tile, start),
        grid_spec=pltpu.PrefetchScalarGridSpec(
            num_scalar_prefetch=1,
            grid=(steps,),
            in_specs=[whole] * 2
            + [pl.BlockSpec((query.shape[0], tile, dim), lambda i, meta: (0, start + i, 0)) for query in queries],
            out_specs=pl.BlockSpec((tile, heads * dim), lambda i, meta: (i, 0)),
            scratch_shapes=[
                pltpu.VMEM((2 * row_count, dim), jnp.bfloat16),
                pltpu.VMEM((2 * row_count, 2 * dim), jnp.bfloat16),
                pltpu.VMEM((heads, tile, 2 * dim), jnp.float32),
            ],
        ),
        out_shape=jax.ShapeDtypeStruct((steps * tile, heads * dim), jnp.bfloat16),
        compiler_params=pltpu.CompilerParams(vmem_limit_bytes=VMEM_LIMIT),
        cost_estimate=pl.CostEstimate(
            flops=8 * heads * row_count * row_count * dim, bytes_accessed=4 * row_count * dim, transcendentals=0
        ),
    )(meta, own, far, *queries)


def output_kernel(kept_rows, sent_rows, *rest):
    *shards, kept, sent = rest
    columns = shards[0].shape[1]
    for rows, out in ((sent_rows, sent), (kept_rows, kept)):
        for index, shard in enumerate(shards):
            product = jnp.dot(rows[...], shard[...], preferred_element_type=jnp.float32)
            here = slice(index * columns, (index + 1) * columns)
            out[:, :, here] = product.astype(jnp.bfloat16).reshape(*out.shape[:2], -1)


def output_part(kept_rows, sent_rows, tile, shards):
    rows, depth = kept_rows.shape
    width = len(shards) * shards[0].shape[1]

    def whole(shape):
        return pl.BlockSpec(shape, lambda n: (0,) * len(shape))

    out = (rows // tile, tile, width)
    return pl.pallas_call(
        output_kernel,
        grid=(1,),
        in_specs=[whole((rows, depth))] * 2 + [whole(shards[0].shape)] * len(shards),
        out_specs=[whole(out)] * 2,
        out_shape=[jax.ShapeDtypeStruct(out, jnp.bfloat16)] * 2,
        compiler_params=pltpu.CompilerParams(vmem_limit_bytes=VMEM_LIMIT),
        cost_estimate=pl.CostEstimate(flops=12 * rows * width * depth, bytes_accessed=8 * rows * width, transcendentals=0),
    )(kept_rows, sent_rows, *shards)


def finish_kernel(columns, meta, states, gain, *rest):
    *terms, hidden_out, normed_out = rest
    index = 0
    for kept, arrived in zip(terms[::2], terms[1::2]):
        for part in range(kept.shape[1] // columns):
            here = slice(part * columns, (part + 1) * columns)
            there = pl.ds(pl.multiple_of(meta[index] * columns, columns), columns)
            total = kept[:, here].astype(jnp.float32) + arrived[:, here].astype(jnp.float32)
            hidden_out[:, there] = (states[:, there].astype(jnp.float32) + total).astype(jnp.bfloat16)
            index += 1
    hidden = hidden_out[...].astype(jnp.float32)
    inverse = lax.rsqrt(jnp.mean(hidden * hidden, axis=-1, keepdims=True) + epsilon)
    normed_out[...] = (hidden * inverse * gain[...]).astype(jnp.bfloat16)


def finish(meta, states, gain, terms, columns):
    rows, width = states.shape
    tile = min(64, rows)

    def block(wide):
        return pl.BlockSpec((tile, wide), lambda i, meta: (i, 0))

    return pl.pallas_call(
        functools.partial(finish_kernel, columns),
        grid_spec=pltpu.PrefetchScalarGridSpec(
            num_scalar_prefetch=1,
            grid=(rows // tile,),
            in_specs=[block(width), pl.BlockSpec((1, width), lambda i, meta: (0, 0))]
            + [block(term.shape[1]) for term in terms],
            out_specs=[block(width)] * 2,
        ),
        out_shape=[jax.ShapeDtypeStruct((rows, width), jnp.bfloat16)] * 2,
        compiler_params=pltpu.CompilerParams(vmem_limit_bytes=VMEM_LIMIT),
        cost_estimate=FREE,
    )(meta, states, gain[None, :], *terms)


def per_device(
    hidden_in,
    norm_attention,
    norm_experts,
    query_master,
    trainer_key_value_weight,
    output_master,
    query_gain,
    key_gain,
    lengths,
    router,
    expert_gateup,
    expert_down,
    routes,
):
    experts_axis = lax.axis_size("expert")
    group_member = lax.axis_index("expert")
    group_index = lax.axis_index("group")
    heads = QUERY_HEADS // experts_axis
    dim = HEAD_DIMENSION
    rows_here, model_width = hidden_in.shape
    local_rows = rows_here * experts_axis

    groups = lax.axis_size("group")
    place, side = group_index // 2, group_index % 2
    common_head = group_member * heads // (QUERY_HEADS // KEY_VALUE_HEADS)
    pair = lax.dynamic_slice_in_dim(trainer_key_value_weight, common_head * dim, dim, 2)
    joined = jnp.concatenate([pair[0], pair[1], query_master], axis=1).astype(jnp.bfloat16)
    output_here = output_master.astype(jnp.bfloat16)
    joined_rounds = Beside(joined)
    normed = norm_rows(after(hidden_in, joined), norm_attention).astype(jnp.bfloat16)
    blocks = gather_tokens(normed)
    parity = after(side, joined_rounds.token())
    output_here = after(output_here, joined_rounds.token())
    output_crossed = cross(output_here)
    joined_rounds.round()
    query_gain, key_gain, lengths, routes = lax.optimization_barrier(
        (query_gain, key_gain, lengths, routes, joined_rounds.token())
    )[:4]
    joined_rounds.round()
    output_here, output_crossed = lax.optimization_barrier(
        (output_here, output_crossed, joined_rounds.token())
    )[:2]
    output_rounds = Beside(output_here, output_crossed)
    joined_rounds.round()
    shards = joined_rounds.held(range(groups))
    output_rounds.round(joined_rounds.token())

    masks = doubling_masks(experts_axis)
    block_order = jnp.bitwise_xor(group_member, jnp.array(masks, jnp.int32))
    meta = jnp.concatenate([jnp.stack([place, side]), held_groups(place, side), block_order]).astype(jnp.int32)

    inside = routes < experts_axis
    expert_window = jnp.sum(jnp.where(inside, routes, 0), axis=1)
    present = jnp.any(inside, axis=1)
    capacity = local_rows // (experts_axis * experts_axis)
    member_table = (present[:, None] & (expert_window[:, None] == block_order[None, :])).astype(jnp.int32)
    ranking = jnp.cumsum(member_table, axis=0) - 1
    slot_index = jnp.sum(member_table * (ranking + jnp.arange(experts_axis) * capacity), axis=1)
    select = (
        (jnp.arange(experts_axis * capacity)[:, None] == slot_index[None, :]) & present[None, :]
    ).astype(jnp.bfloat16)

    own_places = local_positions(parity, local_rows).astype(jnp.float32)
    exponents = jnp.arange(dim // 2).astype(jnp.float32)
    inverse = jnp.exp(exponents * (-2.0 * math.log(rope_theta) / dim))
    angles = own_places[:, None] * inverse[None, :]
    cosine_values, sine_values = jnp.cos(angles), jnp.sin(angles)
    cosine = jnp.concatenate([cosine_values, cosine_values], axis=1)
    sine = jnp.concatenate([-sine_values, sine_values], axis=1)

    def tables(gain):
        return cosine * gain, sine * jnp.roll(gain, dim // 2)

    lanes = jnp.arange(dim)
    swap = (lanes[:, None] == (lanes[None, :] + dim // 2) % dim).astype(jnp.float32)
    nothing = jnp.zeros((dim, dim), jnp.float32)
    mixer = jnp.block([[swap, nothing], [nothing, nothing + 1.0 / dim]]).astype(jnp.bfloat16)
    query_tables = tables(query_gain * (dim**-0.5 * math.log2(math.e)))
    key_tables = tables(key_gain)
    blocks[0] = after(blocks[0], select)
    own_pair = project(key_kernel, 0, 1, meta, blocks, shards, *key_tables, mixer)
    far_pair = cross(own_pair)
    rows_now = [after(blocks[0], own_pair)] + blocks[1:]
    queries = [project(query_kernel, 1, heads // 2, meta, rows_now, shards, *query_tables, mixer)]
    queries[0] = after(queries[0], output_rounds.token())
    output_rounds.round(queries[0], far_pair)

    valid_length = jnp.sum(jnp.where(jnp.arange(lengths.shape[0]) == group_index // 2, lengths, 0))
    attend_meta = jnp.concatenate([jnp.stack([parity, valid_length]), block_order]).astype(jnp.int32)
    sent_rows = attend(attend_meta, queries, own_pair, far_pair, rows_here, 1)
    queries[0] = after(queries[0], output_rounds.token())
    output_rounds.round(sent_rows)
    kept_rows = attend(attend_meta, queries, own_pair, far_pair, rows_here, 0)

    order = [0, 1, 2, 4, 5, 3, 6, 7] if groups == 8 else list(range(groups))
    cut = groups * 5 // 8
    output_shards = output_rounds.held(order)
    terms = []
    for part in (output_shards[:cut], output_shards[cut:]):
        both, _ = scatter_sum(*output_part(kept_rows, sent_rows, rows_here, part))
        terms += both
    finish_meta = jnp.stack([meta[2 + i] for i in order])
    hidden, normed_second = finish(finish_meta, hidden_in, norm_experts, terms, output_here.shape[1])

    logits = jnp.dot(normed_second, router, preferred_element_type=jnp.float32)
    route_table = routes[:, :, None] == jnp.arange(logits.shape[1])[None, None, :]
    picked = jnp.sum(jnp.where(route_table, logits[:, None, :], 0.0), axis=-1)
    raised = jnp.exp(picked)
    gate_values = raised / jnp.sum(raised, axis=1, keepdims=True)
    gate_window = jnp.sum(jnp.where(inside, gate_values, 0.0), axis=1)
    outgoing = (
        jnp.dot(select, normed_second, preferred_element_type=jnp.float32)
        .astype(jnp.bfloat16)
        .reshape(experts_axis, capacity, model_width)
    )

    def exchange(slots):
        return jnp.stack([slots[0]] + [from_xor(slots[j], "expert", masks[j]) for j in range(1, experts_axis)])

    gateup_here = expert_gateup[0]
    down_here = expert_down[0]
    hidden_units = down_here.shape[0]
    slot_items = exchange(outgoing)
    flattened = slot_items.reshape(-1, slot_items.shape[-1])
    gate_up = jnp.dot(flattened, gateup_here, preferred_element_type=jnp.float32)
    active = (jax.nn.silu(gate_up[:, :hidden_units]) * gate_up[:, hidden_units:]).astype(
        jnp.bfloat16
    )
    result = (
        jnp.dot(active, down_here, preferred_element_type=jnp.float32)
        .astype(jnp.bfloat16)
        .reshape(slot_items.shape)
    )
    returned = exchange(result)
    combined = jnp.dot(
        jnp.transpose(select), returned.reshape(-1, model_width), preferred_element_type=jnp.float32
    )
    expert_mix = (gate_window[:, None] * combined).astype(jnp.bfloat16)
    return (hidden, expert_mix)


def solution(mesh):
    return jax.shard_map(
        per_device,
        mesh=mesh,
        in_specs=(
            P(("group", "expert"), None),
            P(),
            P(),
            P("group", "expert"),
            P(None, "group", None),
            P("expert", "group"),
            P(),
            P(),
            P(),
            P(),
            P("expert", None, None),
            P("expert", None, None),
            P(("group", "expert"), None),
        ),
        out_specs=(P(("group", "expert"), None), P(("group", "expert"), None)),
        check_vma=False,
    )
```

```python
import functools
import math

import jax
import jax.numpy as jnp
from jax import lax
from jax.experimental import pallas as pl
from jax.experimental.pallas import tpu as pltpu
from jax.sharding import PartitionSpec as P

QUERY_HEADS = 32
KEY_VALUE_HEADS = 4
HEAD_DIMENSION = 128

epsilon = 1e-06
rope_theta = 1000000.0
VMEM_LIMIT = 32 * 1024 * 1024
FREE = pl.CostEstimate(flops=0, bytes_accessed=0, transcendentals=0)


def norm_rows(values, gain_vector):
    widened = values.astype(jnp.float32)
    inverse_rms = lax.rsqrt(jnp.mean(widened * widened, axis=-1, keepdims=True) + epsilon)
    return widened * inverse_rms * gain_vector


def local_positions(parity, row_count):
    indices = jnp.arange(row_count)
    quarter = row_count // 2
    offset = jnp.where(parity == 0, jnp.where(indices < quarter, 0, 2 * quarter), quarter)
    return indices + offset


def from_xor(block, axis, mask):
    count = lax.axis_size(axis)
    return lax.ppermute(block, axis, [(i, i ^ mask) for i in range(count)])


def cross(block):
    return from_xor(block, "group", 1)


def after(block, *others):
    return lax.optimization_barrier((block, *others))[0]


LINE = ((0, 1, 2, 3), (1, 0, 2, 3), (2, 3, 1, 0), (3, 2, 1, 0))
PAIRS = ((0, 1), (1, 0), (2, 3), (3, 2))
MIDDLE = ((1, 2), (2, 1))
OUTWARD = ((1, 0), (2, 3))


def along(block, moves):
    return lax.ppermute(block, "group", [(2 * a + s, 2 * b + s) for a, b in moves for s in range(2)])


def line_rounds(block, shards, crossed, head):
    place = lax.axis_index("group") // 2
    edge = (place == 0) | (place == 3)
    shards[0] = block
    if crossed is None:
        shards[1], inner, shards[4] = yield along(block, PAIRS), along(block, MIDDLE), cross(block[head:])
    else:
        shards[4] = crossed
        shards[1], inner = yield along(block, PAIRS), along(block, MIDDLE)
    shards[5], inner_far, outer = yield cross(shards[1][head:]), along(shards[1], MIDDLE), along(inner, OUTWARD)
    shards[2] = jnp.where(edge, outer, inner)
    shards[6], outer = yield cross(shards[2][head:]), along(inner_far, OUTWARD)
    shards[3] = jnp.where(edge, outer, inner_far)
    (shards[7],) = yield (cross(shards[3][head:]),)
    yield ()


class Beside:
    def __init__(self, block, crossed=None, head=0):
        groups = lax.axis_size("group")
        self.found = [None] * groups if groups == 8 else list(lax.all_gather(block, "group"))
        self.chain = line_rounds(block, self.found, crossed, head) if groups == 8 else None
        self.brought = (block,) if self.chain is None else lax.optimization_barrier(next(self.chain))

    def round(self, *ready):
        if self.chain is not None:
            results = after(self.brought, *ready)
            self.brought = lax.optimization_barrier(self.chain.send(results))

    def token(self):
        return self.brought[0]

    def held(self, indices):
        if self.chain is not None and any(self.found[index] is None for index in indices):
            self.chain.send(self.brought)
            self.chain = None
        return [self.found[index] for index in indices]


def held_groups(place, side):
    groups = lax.axis_size("group")
    if groups != 8:
        return jnp.arange(groups)
    places = jnp.sum(jnp.where(jnp.arange(4)[:, None] == place, jnp.array(LINE, jnp.int32), 0), axis=0)
    return jnp.concatenate([2 * places + side, 2 * places + 1 - side])


def doubling_masks(count):
    masks, stride = [0], count // 2
    while stride:
        masks = masks + [mask ^ stride for mask in masks]
        stride //= 2
    return masks


def gather_tokens(rows):
    blocks = [rows]
    stride = lax.axis_size("expert") // 2
    while stride:
        blocks = blocks + [from_xor(block, "expert", stride) for block in blocks]
        stride //= 2
    return blocks


def sum_terms(terms):
    return functools.reduce(jnp.add, [term.astype(jnp.float32) for term in terms]).astype(jnp.bfloat16)


def scatter_rest(kept, sent):
    stride = 2
    while True:
        kept = [*kept, from_xor(sent, "expert", stride)]
        half = sent.shape[0] // 2
        if not half:
            return [term[0] for term in kept]
        whole = sum_terms(kept)
        kept, sent = [whole[:half]], whole[half:]
        stride *= 2


def stack_shards(meta, refs, weights):
    depth = weights.shape[0] // len(refs)
    for index, ref in enumerate(refs):
        weights[pl.ds(pl.multiple_of(meta[2 + index] * depth, depth), depth), :] = ref[...]


def pack_kernel(meta, query, pair, out):
    dim = HEAD_DIMENSION
    out[:, :dim] = pair[0].astype(jnp.bfloat16)
    out[:, dim : 2 * dim] = pair[1].astype(jnp.bfloat16)
    out[:, 2 * dim :] = query[...].astype(jnp.bfloat16)


def pack(head, query, pair):
    rows, columns = query.shape
    dim = HEAD_DIMENSION
    tile = min(64, rows)
    return pl.pallas_call(
        pack_kernel,
        grid_spec=pltpu.PrefetchScalarGridSpec(
            num_scalar_prefetch=1,
            grid=(rows // tile,),
            in_specs=[
                pl.BlockSpec((tile, columns), lambda i, meta: (i, 0)),
                pl.BlockSpec((2, tile, dim), lambda i, meta: (0, i, meta[0])),
            ],
            out_specs=pl.BlockSpec((tile, columns + 2 * dim), lambda i, meta: (i, 0)),
        ),
        out_shape=jax.ShapeDtypeStruct((rows, columns + 2 * dim), jnp.bfloat16),
        compiler_params=pltpu.CompilerParams(vmem_limit_bytes=VMEM_LIMIT),
        cost_estimate=FREE,
    )(head, query, pair)


def turn(values, cosines, sines, mixer):
    values = values.astype(jnp.bfloat16)
    wide = values.astype(jnp.float32)
    both = jnp.concatenate([values, (wide * wide).astype(jnp.bfloat16)], axis=1)
    mixed = jnp.dot(both, mixer, preferred_element_type=jnp.float32)
    dim = values.shape[1]
    inverse = lax.rsqrt(mixed[:, dim:] + epsilon)
    return ((wide * cosines + mixed[:, :dim] * sines) * inverse).astype(jnp.bfloat16)


def query_kernel(count, meta, *rest):
    rows, (cosine, sine, mixer, *rest) = rest[:count], rest[count:]
    *shards, query_out, weights, joined = rest
    stack_shards(meta, shards, weights)
    tile, dim = rows[0].shape[0], HEAD_DIMENSION

    @pl.when(pl.program_id(0) == 0)
    def _():
        for index, block in enumerate(rows):
            joined[index * tile : (index + 1) * tile, :] = block[...]

    projected = jnp.dot(joined[...], weights[...], preferred_element_type=jnp.float32)
    for block in range(count):
        spot = pl.ds(pl.multiple_of(meta[2 + len(shards) + block] * tile, tile), tile)
        here = slice(block * tile, (block + 1) * tile)
        for head in range(2):
            query_out[head, here, :] = turn(
                projected[here, head * dim : (head + 1) * dim], cosine[spot, :], sine[spot, :], mixer[...]
            )


def key_kernel(count, meta, *rest):
    rows, (cosine, sine, mixer, *rest) = rest[:count], rest[count:]
    *shards, pair_out, weights, joined = rest
    stack_shards(meta, shards, weights)
    tile, dim = rows[0].shape[0], HEAD_DIMENSION

    @pl.when(pl.program_id(0) == 0)
    def _():
        for index, block in enumerate(rows):
            joined[index * tile : (index + 1) * tile, :] = block[...]

    projected = jnp.dot(joined[...], weights[...], preferred_element_type=jnp.float32)
    for block in range(count):
        spot = pl.ds(pl.multiple_of(meta[2 + len(shards) + block] * tile, tile), tile)
        here = slice(block * tile, (block + 1) * tile)
        pair_out[0, spot, :] = turn(projected[here, :dim], cosine[spot, :], sine[spot, :], mixer[...])
        pair_out[1, spot, :] = projected[here, dim:].astype(jnp.bfloat16)


def project(kernel, first, steps, meta, blocks, shards, cosine, sine, mixer):
    count, (tile, width) = len(blocks), blocks[0].shape
    dim = HEAD_DIMENSION
    shard = pl.BlockSpec((shards[0].shape[0], 2 * dim), lambda n, meta: (0, first + n))
    table = pl.BlockSpec((count * tile, dim), lambda n, meta: (0, 0))
    return pl.pallas_call(
        functools.partial(kernel, count),
        grid_spec=pltpu.PrefetchScalarGridSpec(
            num_scalar_prefetch=1,
            grid=(steps,),
            in_specs=[pl.BlockSpec((tile, width), lambda n, meta: (0, 0))] * count
            + [
                table,
                table,
                pl.BlockSpec((2 * dim, 2 * dim), lambda n, meta: (0, 0)),
            ]
            + [shard] * len(shards),
            out_specs=pl.BlockSpec((2, count * tile, dim), lambda n, meta: (n, 0, 0)),
            scratch_shapes=[
                pltpu.VMEM((width, 2 * dim), jnp.bfloat16),
                pltpu.VMEM((count * tile, width), jnp.bfloat16),
            ],
        ),
        out_shape=jax.ShapeDtypeStruct((2 * steps, count * tile, dim), jnp.bfloat16),
        compiler_params=pltpu.CompilerParams(vmem_limit_bytes=VMEM_LIMIT),
        cost_estimate=pl.CostEstimate(
            flops=16 * steps * count * tile * width * dim, bytes_accessed=2 * count * tile * width, transcendentals=0
        ),
    )(meta, *blocks, cosine, sine, mixer, *shards)


def attend_kernel(tile, block_of, meta, own, far, *rest):
    *queries, out, keys, values, total = rest
    heads, dim = total.shape[0], HEAD_DIMENSION
    query = [part.at[head] for part in queries for head in range(part.shape[0])]
    row_count = own.shape[1]
    half = row_count // 2
    parity, length = meta[0], meta[1]
    step = pl.program_id(0)

    @pl.when(step == 0)
    def _():
        ones = jnp.ones((half, dim), jnp.bfloat16)
        for pair, whose in ((own, parity), (far, 1 - parity)):
            for part in range(2):
                base = jnp.where(whose == 0, 3 * half * part, half * (1 + part))
                base = pl.multiple_of(base, half)
                source = pl.ds(part * half, half)
                keys[pl.ds(base, half), :] = pair[0, source, :]
                valid = base + lax.broadcasted_iota(jnp.int32, (half, dim), 0) < length
                zero = jnp.zeros((half, dim), jnp.bfloat16)
                values[pl.ds(base, half), :dim] = jnp.where(valid, pair[1, source, :], zero)
                values[pl.ds(base, half), dim:] = jnp.where(valid, ones, zero)

    first = meta[2 + block_of(step)] * tile
    first = first + jnp.where(parity == 0, jnp.where(first < half, 0, 2 * half), half)

    def weigh(head, start, width, masked):
        scores = lax.dot_general(
            query[head][...], keys[pl.ds(start, width), :], (((1,), (1,)), ((), ())),
            preferred_element_type=jnp.float32,
        )
        weights = jnp.exp2(scores)
        if masked:
            below = lax.broadcasted_iota(jnp.int32, weights.shape, 1) <= lax.broadcasted_iota(
                jnp.int32, weights.shape, 0
            )
            weights = jnp.where(below, weights, 0.0)
        return jnp.dot(
            weights.astype(jnp.bfloat16), values[pl.ds(start, width), :], preferred_element_type=jnp.float32
        )

    diagonal = pl.multiple_of(first, tile)
    for head in range(heads):
        total[head] = weigh(head, diagonal, tile, True)

    def wide(index, _):
        start = pl.multiple_of(index * half, half)
        for head in range(heads):
            total[head] += weigh(head, start, half, False)
        return 0

    lax.fori_loop(0, first // half, wide, 0)

    def narrow(index, _):
        start = pl.multiple_of(index * tile, tile)
        for head in range(heads):
            total[head] += weigh(head, start, tile, False)
        return 0

    lax.fori_loop(first // half * (half // tile), first // tile, narrow, 0)
    for head in range(heads):
        summed = total[head]
        out[:, head * dim : (head + 1) * dim] = (summed[:, :dim] / summed[:, dim:]).astype(jnp.bfloat16)


def attend(meta, queries, own, far, tile, part):
    _, row_count, dim = queries[0].shape
    heads = sum(query.shape[0] for query in queries)
    steps = row_count // tile // 2

    def block_of(step):
        return step + steps // 2 * (part + (step >= steps // 2))

    whole = pl.BlockSpec((2, row_count, dim), lambda i, meta: (0, 0, 0))
    return pl.pallas_call(
        functools.partial(attend_kernel, tile, block_of),
        grid_spec=pltpu.PrefetchScalarGridSpec(
            num_scalar_prefetch=1,
            grid=(steps,),
            in_specs=[whole] * 2
            + [pl.BlockSpec((query.shape[0], tile, dim), lambda i, meta: (0, block_of(i), 0)) for query in queries],
            out_specs=pl.BlockSpec((tile, heads * dim), lambda i, meta: (i, 0)),
            scratch_shapes=[
                pltpu.VMEM((2 * row_count, dim), jnp.bfloat16),
                pltpu.VMEM((2 * row_count, 2 * dim), jnp.bfloat16),
                pltpu.VMEM((heads, tile, 2 * dim), jnp.float32),
            ],
        ),
        out_shape=jax.ShapeDtypeStruct((steps * tile, heads * dim), jnp.bfloat16),
        compiler_params=pltpu.CompilerParams(vmem_limit_bytes=VMEM_LIMIT),
        cost_estimate=pl.CostEstimate(
            flops=8 * heads * row_count * row_count * dim, bytes_accessed=4 * row_count * dim, transcendentals=0
        ),
    )(meta, own, far, *queries)


def output_kernel(plan, meta, rows, *rest):
    *shards, kept, sent = rest
    columns = shards[0].shape[1]
    half = rows.shape[0] // 2
    for index, pieces in enumerate(plan):
        here = pl.ds(pl.multiple_of(meta[index] * columns, columns), columns)
        for part, out in enumerate((kept, sent)):
            product = 0.0
            for shard, start, size, depth in pieces:
                left = rows[part * half : (part + 1) * half, depth : depth + size]
                right = shards[shard][start : start + size, :]
                product += jnp.dot(left, right, preferred_element_type=jnp.float32)
            out[:, :, here] = product.astype(jnp.bfloat16).reshape(*out.shape[:2], columns)


def output_part(plan, meta, rows, tile, shards):
    count, depth = rows.shape
    width = len(plan) * shards[0].shape[1]

    def whole(shape):
        return pl.BlockSpec(shape, lambda n, meta: (0,) * len(shape))

    out = (count // 2 // tile, tile, width)
    return pl.pallas_call(
        functools.partial(output_kernel, plan),
        grid_spec=pltpu.PrefetchScalarGridSpec(
            num_scalar_prefetch=1,
            grid=(1,),
            in_specs=[whole((count, depth))] + [whole(shard.shape) for shard in shards],
            out_specs=[whole(out)] * 2,
        ),
        out_shape=[jax.ShapeDtypeStruct(out, jnp.bfloat16)] * 2,
        compiler_params=pltpu.CompilerParams(vmem_limit_bytes=VMEM_LIMIT),
        cost_estimate=FREE,
    )(meta, rows, *shards)


def finish_kernel(states, gain, *rest):
    *terms, hidden_out, normed_out = rest
    total = functools.reduce(jnp.add, [term[...].astype(jnp.float32) for term in terms])
    rounded = (states[...].astype(jnp.float32) + total).astype(jnp.bfloat16)
    hidden_out[...] = rounded
    hidden = rounded.astype(jnp.float32)
    inverse = lax.rsqrt(jnp.mean(hidden * hidden, axis=-1, keepdims=True) + epsilon)
    normed_out[...] = (hidden * inverse * gain[...]).astype(jnp.bfloat16)


def finish(states, gain, terms):
    rows, width = states.shape
    tile = min(64, rows)
    block = pl.BlockSpec((tile, width), lambda i: (i, 0))
    return pl.pallas_call(
        finish_kernel,
        grid=(rows // tile,),
        in_specs=[block, pl.BlockSpec((1, width), lambda i: (0, 0))] + [block] * len(terms),
        out_specs=[block] * 2,
        out_shape=[jax.ShapeDtypeStruct((rows, width), jnp.bfloat16)] * 2,
        compiler_params=pltpu.CompilerParams(vmem_limit_bytes=VMEM_LIMIT),
        cost_estimate=FREE,
    )(states, gain[None, :], *terms)


def per_device(
    hidden_in,
    norm_attention,
    norm_experts,
    query_master,
    trainer_key_value_weight,
    output_master,
    query_gain,
    key_gain,
    lengths,
    router,
    expert_gateup,
    expert_down,
    routes,
):
    experts_axis = lax.axis_size("expert")
    group_member = lax.axis_index("expert")
    group_index = lax.axis_index("group")
    heads = QUERY_HEADS // experts_axis
    dim = HEAD_DIMENSION
    rows_here, model_width = hidden_in.shape
    local_rows = rows_here * experts_axis

    groups = lax.axis_size("group")
    place, side = group_index // 2, group_index % 2
    common_head = group_member * heads // (QUERY_HEADS // KEY_VALUE_HEADS)
    joined = pack(common_head.astype(jnp.int32).reshape(1), query_master, trainer_key_value_weight)
    output_here = output_master.astype(jnp.bfloat16)
    joined_rounds = Beside(joined)
    normed = norm_rows(after(hidden_in, joined), norm_attention).astype(jnp.bfloat16)
    blocks = gather_tokens(normed)
    parity = after(side, joined_rounds.token())
    output_here = after(output_here, joined_rounds.token())
    output_crossed = cross(output_here)
    joined_rounds.round()
    query_gain, key_gain, lengths, routes = lax.optimization_barrier(
        (query_gain, key_gain, lengths, routes, joined_rounds.token())
    )[:4]
    joined_rounds.round()
    output_here, output_crossed = lax.optimization_barrier(
        (output_here, output_crossed, joined_rounds.token())
    )[:2]
    depth = output_here.shape[0]
    if groups == 8:
        first = depth // 4
        rest = depth - first
        output_block = jnp.concatenate([output_here[:first], output_crossed[:first], output_here[first:]], axis=0)
        output_rounds = Beside(output_block, output_crossed[first:], 2 * first)
        plan = [((k, 0, first, 0), (k, 2 * first, rest, first)) for k in range(4)]
        plan += [((k, first, first, 0), (4 + k, 0, rest, first)) for k in range(4)]
    else:
        output_rounds = Beside(output_here)
        plan = [((k, 0, depth, 0),) for k in range(groups)]
    joined_rounds.round()
    shards = joined_rounds.held(range(groups))
    output_rounds.round(joined_rounds.token())

    masks = doubling_masks(experts_axis)
    block_order = jnp.bitwise_xor(group_member, jnp.array(masks, jnp.int32))
    meta = jnp.concatenate([jnp.stack([place, side]), held_groups(place, side), block_order]).astype(jnp.int32)

    inside = routes < experts_axis
    expert_window = jnp.sum(jnp.where(inside, routes, 0), axis=1)
    present = jnp.any(inside, axis=1)
    capacity = local_rows // (experts_axis * experts_axis)
    member_table = (present[:, None] & (expert_window[:, None] == block_order[None, :])).astype(jnp.int32)
    ranking = jnp.cumsum(member_table, axis=0) - 1
    slot_index = jnp.sum(member_table * (ranking + jnp.arange(experts_axis) * capacity), axis=1)
    select = (
        (jnp.arange(experts_axis * capacity)[:, None] == slot_index[None, :]) & present[None, :]
    ).astype(jnp.bfloat16)

    own_places = local_positions(parity, local_rows).astype(jnp.float32)
    exponents = jnp.arange(dim // 2).astype(jnp.float32)
    inverse = jnp.exp(exponents * (-2.0 * math.log(rope_theta) / dim))
    angles = own_places[:, None] * inverse[None, :]
    cosine_values, sine_values = jnp.cos(angles), jnp.sin(angles)
    cosine = jnp.concatenate([cosine_values, cosine_values], axis=1)
    sine = jnp.concatenate([-sine_values, sine_values], axis=1)

    def tables(gain):
        return cosine * gain, sine * jnp.roll(gain, dim // 2)

    lanes = jnp.arange(dim)
    swap = (lanes[:, None] == (lanes[None, :] + dim // 2) % dim).astype(jnp.float32)
    nothing = jnp.zeros((dim, dim), jnp.float32)
    mixer = jnp.block([[swap, nothing], [nothing, nothing + 1.0 / dim]]).astype(jnp.bfloat16)
    query_tables = tables(query_gain * (dim**-0.5 * math.log2(math.e)))
    key_tables = tables(key_gain)
    blocks[0] = after(blocks[0], select)
    own_pair = project(key_kernel, 0, 1, meta, blocks, shards, *key_tables, mixer)
    far_pair = cross(own_pair)
    rows_now = [after(blocks[0], own_pair)] + blocks[1:]
    queries = [project(query_kernel, 1, heads // 2, meta, rows_now, shards, *query_tables, mixer)]
    queries[0] = after(queries[0], output_rounds.token())
    output_rounds.round(queries[0], far_pair)

    valid_length = jnp.sum(jnp.where(jnp.arange(lengths.shape[0]) == group_index // 2, lengths, 0))
    attend_meta = jnp.concatenate([jnp.stack([parity, valid_length]), block_order]).astype(jnp.int32)
    next_rows = attend(attend_meta, queries, own_pair, far_pair, rows_here, 1)
    queries[0] = after(queries[0], output_rounds.token())
    output_rounds.round(next_rows)
    last_rows = attend(attend_meta, queries, own_pair, far_pair, rows_here, 0)

    output_shards = output_rounds.held(range(groups))
    next_rows = after(next_rows, last_rows)
    output_meta = held_groups(place, side).astype(jnp.int32)
    kept, sent = output_part(plan, output_meta, next_rows, rows_here, output_shards)
    next_sum = sum_terms([kept, from_xor(sent, "expert", 1)])
    kept, sent = output_part(plan, output_meta, last_rows, rows_here, output_shards)
    terms = scatter_rest([kept, from_xor(sent, "expert", 1)], next_sum)
    hidden, normed_second = finish(hidden_in, norm_experts, terms)

    logits = jnp.dot(normed_second, router, preferred_element_type=jnp.float32)
    route_table = routes[:, :, None] == jnp.arange(logits.shape[1])[None, None, :]
    picked = jnp.sum(jnp.where(route_table, logits[:, None, :], 0.0), axis=-1)
    raised = jnp.exp(picked)
    gate_values = raised / jnp.sum(raised, axis=1, keepdims=True)
    gate_window = jnp.sum(jnp.where(inside, gate_values, 0.0), axis=1)
    outgoing = (
        jnp.dot(select, normed_second, preferred_element_type=jnp.float32)
        .astype(jnp.bfloat16)
        .reshape(experts_axis, capacity, model_width)
    )

    def exchange(slots):
        return jnp.stack([slots[0]] + [from_xor(slots[j], "expert", masks[j]) for j in range(1, experts_axis)])

    gateup_here = expert_gateup[0]
    down_here = expert_down[0]
    hidden_units = down_here.shape[0]
    slot_items = exchange(outgoing)
    flattened = slot_items.reshape(-1, slot_items.shape[-1])
    gate_up = jnp.dot(flattened, gateup_here, preferred_element_type=jnp.float32)
    active = (jax.nn.silu(gate_up[:, :hidden_units]) * gate_up[:, hidden_units:]).astype(
        jnp.bfloat16
    )
    result = (
        jnp.dot(active, down_here, preferred_element_type=jnp.float32)
        .astype(jnp.bfloat16)
        .reshape(slot_items.shape)
    )
    returned = exchange(result)
    combined = jnp.dot(
        jnp.transpose(select), returned.reshape(-1, model_width), preferred_element_type=jnp.float32
    )
    expert_mix = (gate_window[:, None] * combined).astype(jnp.bfloat16)
    return (hidden, expert_mix)


def solution(mesh):
    return jax.shard_map(
        per_device,
        mesh=mesh,
        in_specs=(
            P(("group", "expert"), None),
            P(),
            P(),
            P("group", "expert"),
            P(None, "group", None),
            P("expert", "group"),
            P(),
            P(),
            P(),
            P(),
            P("expert", None, None),
            P("expert", None, None),
            P(("group", "expert"), None),
        ),
        out_specs=(P(("group", "expert"), None), P(("group", "expert"), None)),
        check_vma=False,
    )
```

```python
import functools
import math

import jax
import jax.numpy as jnp
from jax import lax
from jax.experimental import pallas as pl
from jax.experimental.pallas import tpu as pltpu
from jax.sharding import PartitionSpec as P

QUERY_HEADS = 32
KEY_VALUE_HEADS = 4
HEAD_DIMENSION = 128

epsilon = 1e-06
rope_theta = 1000000.0
VMEM_LIMIT = 32 * 1024 * 1024
FREE = pl.CostEstimate(flops=0, bytes_accessed=0, transcendentals=0)


def norm_rows(values, gain_vector):
    widened = values.astype(jnp.float32)
    inverse_rms = lax.rsqrt(jnp.mean(widened * widened, axis=-1, keepdims=True) + epsilon)
    return widened * inverse_rms * gain_vector


def local_positions(parity, row_count):
    indices = jnp.arange(row_count)
    quarter = row_count // 2
    offset = jnp.where(parity == 0, jnp.where(indices < quarter, 0, 2 * quarter), quarter)
    return indices + offset


def from_xor(block, axis, mask):
    count = lax.axis_size(axis)
    return lax.ppermute(block, axis, [(i, i ^ mask) for i in range(count)])


def cross(block):
    return from_xor(block, "group", 1)


def after(block, *others):
    return lax.optimization_barrier((block, *others))[0]


LINE = ((0, 1, 2, 3), (1, 0, 2, 3), (2, 3, 1, 0), (3, 2, 1, 0))
PAIRS = ((0, 1), (1, 0), (2, 3), (3, 2))
MIDDLE = ((1, 2), (2, 1))
OUTWARD = ((1, 0), (2, 3))


def along(block, moves):
    return lax.ppermute(block, "group", [(2 * a + s, 2 * b + s) for a, b in moves for s in range(2)])


def line_rounds(block, shards, crossed, head):
    place = lax.axis_index("group") // 2
    edge = (place == 0) | (place == 3)
    shards[0] = block
    if crossed is None:
        shards[1], inner, shards[4] = yield along(block, PAIRS), along(block, MIDDLE), cross(block[head:])
    else:
        shards[4] = crossed
        shards[1], inner = yield along(block, PAIRS), along(block, MIDDLE)
    shards[5], inner_far, outer = yield cross(shards[1][head:]), along(shards[1], MIDDLE), along(inner, OUTWARD)
    shards[2] = jnp.where(edge, outer, inner)
    shards[6], outer = yield cross(shards[2][head:]), along(inner_far, OUTWARD)
    shards[3] = jnp.where(edge, outer, inner_far)
    (shards[7],) = yield (cross(shards[3][head:]),)
    yield ()


class Beside:
    def __init__(self, block, crossed=None, head=0):
        groups = lax.axis_size("group")
        self.found = [None] * groups if groups == 8 else list(lax.all_gather(block, "group"))
        self.chain = line_rounds(block, self.found, crossed, head) if groups == 8 else None
        self.brought = (block,) if self.chain is None else lax.optimization_barrier(next(self.chain))

    def round(self, *ready):
        if self.chain is not None:
            results = after(self.brought, *ready)
            self.brought = lax.optimization_barrier(self.chain.send(results))

    def token(self):
        return self.brought[0]

    def held(self, indices):
        if self.chain is not None and any(self.found[index] is None for index in indices):
            self.chain.send(self.brought)
            self.chain = None
        return [self.found[index] for index in indices]


def held_groups(place, side):
    groups = lax.axis_size("group")
    if groups != 8:
        return jnp.arange(groups)
    places = jnp.sum(jnp.where(jnp.arange(4)[:, None] == place, jnp.array(LINE, jnp.int32), 0), axis=0)
    return jnp.concatenate([2 * places + side, 2 * places + 1 - side])


def doubling_masks(count):
    masks, stride = [0], count // 2
    while stride:
        masks = masks + [mask ^ stride for mask in masks]
        stride //= 2
    return masks


def gather_tokens(rows):
    blocks = [rows]
    stride = lax.axis_size("expert") // 2
    while stride:
        blocks = blocks + [from_xor(block, "expert", stride) for block in blocks]
        stride //= 2
    return blocks


def sum_terms(terms):
    return functools.reduce(jnp.add, [term.astype(jnp.float32) for term in terms]).astype(jnp.bfloat16)


def scatter_rest(kept, sent):
    stride = 2
    while True:
        kept = [*kept, from_xor(sent, "expert", stride)]
        half = sent.shape[0] // 2
        if not half:
            return [term[0] for term in kept]
        whole = sum_terms(kept)
        kept, sent = [whole[:half]], whole[half:]
        stride *= 2


def stack_shards(meta, refs, weights):
    depth = weights.shape[0] // len(refs)
    for index, ref in enumerate(refs):
        weights[pl.ds(pl.multiple_of(meta[2 + index] * depth, depth), depth), :] = ref[...]


def pack_kernel(meta, query, pair, out):
    dim = HEAD_DIMENSION
    out[:, :dim] = pair[0].astype(jnp.bfloat16)
    out[:, dim : 2 * dim] = pair[1].astype(jnp.bfloat16)
    out[:, 2 * dim :] = query[...].astype(jnp.bfloat16)


def pack(head, query, pair):
    rows, columns = query.shape
    dim = HEAD_DIMENSION
    tile = min(64, rows)
    return pl.pallas_call(
        pack_kernel,
        grid_spec=pltpu.PrefetchScalarGridSpec(
            num_scalar_prefetch=1,
            grid=(rows // tile,),
            in_specs=[
                pl.BlockSpec((tile, columns), lambda i, meta: (i, 0)),
                pl.BlockSpec((2, tile, dim), lambda i, meta: (0, i, meta[0])),
            ],
            out_specs=pl.BlockSpec((tile, columns + 2 * dim), lambda i, meta: (i, 0)),
        ),
        out_shape=jax.ShapeDtypeStruct((rows, columns + 2 * dim), jnp.bfloat16),
        compiler_params=pltpu.CompilerParams(vmem_limit_bytes=VMEM_LIMIT),
        cost_estimate=FREE,
    )(head, query, pair)


def turn(values, cosines, sines, mixer):
    values = values.astype(jnp.bfloat16)
    wide = values.astype(jnp.float32)
    both = jnp.concatenate([values, (wide * wide).astype(jnp.bfloat16)], axis=1)
    mixed = jnp.dot(both, mixer, preferred_element_type=jnp.float32)
    dim = values.shape[1]
    inverse = lax.rsqrt(mixed[:, dim:] + epsilon)
    return ((wide * cosines + mixed[:, :dim] * sines) * inverse).astype(jnp.bfloat16)


def query_kernel(count, meta, *rest):
    rows, (cosine, sine, mixer, *rest) = rest[:count], rest[count:]
    *shards, query_out, weights, joined = rest
    stack_shards(meta, shards, weights)
    tile, dim = rows[0].shape[0], HEAD_DIMENSION

    @pl.when(pl.program_id(0) == 0)
    def _():
        for index, block in enumerate(rows):
            joined[index * tile : (index + 1) * tile, :] = block[...]

    projected = jnp.dot(joined[...], weights[...], preferred_element_type=jnp.float32)
    for block in range(count):
        spot = pl.ds(pl.multiple_of(meta[2 + len(shards) + block] * tile, tile), tile)
        here = slice(block * tile, (block + 1) * tile)
        for head in range(2):
            query_out[head, here, :] = turn(
                projected[here, head * dim : (head + 1) * dim], cosine[spot, :], sine[spot, :], mixer[...]
            )


def key_kernel(count, meta, *rest):
    rows, (cosine, sine, mixer, *rest) = rest[:count], rest[count:]
    *shards, pair_out, weights, joined = rest
    stack_shards(meta, shards, weights)
    tile, dim = rows[0].shape[0], HEAD_DIMENSION

    @pl.when(pl.program_id(0) == 0)
    def _():
        for index, block in enumerate(rows):
            joined[index * tile : (index + 1) * tile, :] = block[...]

    projected = jnp.dot(joined[...], weights[...], preferred_element_type=jnp.float32)
    for block in range(count):
        spot = pl.ds(pl.multiple_of(meta[2 + len(shards) + block] * tile, tile), tile)
        here = slice(block * tile, (block + 1) * tile)
        pair_out[0, spot, :] = turn(projected[here, :dim], cosine[spot, :], sine[spot, :], mixer[...])
        pair_out[1, spot, :] = projected[here, dim:].astype(jnp.bfloat16)


def project(kernel, first, steps, meta, blocks, shards, cosine, sine, mixer):
    count, (tile, width) = len(blocks), blocks[0].shape
    dim = HEAD_DIMENSION
    shard = pl.BlockSpec((shards[0].shape[0], 2 * dim), lambda n, meta: (0, first + n))
    table = pl.BlockSpec((count * tile, dim), lambda n, meta: (0, 0))
    return pl.pallas_call(
        functools.partial(kernel, count),
        grid_spec=pltpu.PrefetchScalarGridSpec(
            num_scalar_prefetch=1,
            grid=(steps,),
            in_specs=[pl.BlockSpec((tile, width), lambda n, meta: (0, 0))] * count
            + [
                table,
                table,
                pl.BlockSpec((2 * dim, 2 * dim), lambda n, meta: (0, 0)),
            ]
            + [shard] * len(shards),
            out_specs=pl.BlockSpec((2, count * tile, dim), lambda n, meta: (n, 0, 0)),
            scratch_shapes=[
                pltpu.VMEM((width, 2 * dim), jnp.bfloat16),
                pltpu.VMEM((count * tile, width), jnp.bfloat16),
            ],
        ),
        out_shape=jax.ShapeDtypeStruct((2 * steps, count * tile, dim), jnp.bfloat16),
        compiler_params=pltpu.CompilerParams(vmem_limit_bytes=VMEM_LIMIT),
        cost_estimate=pl.CostEstimate(
            flops=16 * steps * count * tile * width * dim, bytes_accessed=2 * count * tile * width, transcendentals=0
        ),
    )(meta, *blocks, cosine, sine, mixer, *shards)


def attend_kernel(tile, block_of, meta, own, far, *rest):
    *queries, out, keys, values, total = rest
    heads, dim = total.shape[0], HEAD_DIMENSION
    query = [part.at[head] for part in queries for head in range(part.shape[0])]
    row_count = own.shape[1]
    half = row_count // 2
    parity, length = meta[0], meta[1]
    step = pl.program_id(0)

    @pl.when(step == 0)
    def _():
        ones = jnp.ones((half, dim), jnp.bfloat16)
        for pair, whose in ((own, parity), (far, 1 - parity)):
            for part in range(2):
                base = jnp.where(whose == 0, 3 * half * part, half * (1 + part))
                base = pl.multiple_of(base, half)
                source = pl.ds(part * half, half)
                keys[pl.ds(base, half), :] = pair[0, source, :]
                valid = base + lax.broadcasted_iota(jnp.int32, (half, dim), 0) < length
                zero = jnp.zeros((half, dim), jnp.bfloat16)
                values[pl.ds(base, half), :dim] = jnp.where(valid, pair[1, source, :], zero)
                values[pl.ds(base, half), dim:] = jnp.where(valid, ones, zero)

    first = meta[2 + block_of(step)] * tile
    first = first + jnp.where(parity == 0, jnp.where(first < half, 0, 2 * half), half)

    def weigh(head, start, width, masked):
        scores = lax.dot_general(
            query[head][...], keys[pl.ds(start, width), :], (((1,), (1,)), ((), ())),
            preferred_element_type=jnp.float32,
        )
        weights = jnp.exp2(scores)
        if masked:
            below = lax.broadcasted_iota(jnp.int32, weights.shape, 1) <= lax.broadcasted_iota(
                jnp.int32, weights.shape, 0
            )
            weights = jnp.where(below, weights, 0.0)
        return jnp.dot(
            weights.astype(jnp.bfloat16), values[pl.ds(start, width), :], preferred_element_type=jnp.float32
        )

    diagonal = pl.multiple_of(first, tile)
    for head in range(heads):
        total[head] = weigh(head, diagonal, tile, True)

    def wide(index, _):
        start = pl.multiple_of(index * half, half)
        for head in range(heads):
            total[head] += weigh(head, start, half, False)
        return 0

    lax.fori_loop(0, first // half, wide, 0)

    def narrow(index, _):
        start = pl.multiple_of(index * tile, tile)
        for head in range(heads):
            total[head] += weigh(head, start, tile, False)
        return 0

    lax.fori_loop(first // half * (half // tile), first // tile, narrow, 0)
    for head in range(heads):
        summed = total[head]
        out[:, head * dim : (head + 1) * dim] = (summed[:, :dim] / summed[:, dim:]).astype(jnp.bfloat16)


def attend(meta, queries, own, far, tile, part):
    _, row_count, dim = queries[0].shape
    heads = sum(query.shape[0] for query in queries)
    steps = row_count // tile // 2

    def block_of(step):
        return step + (steps // 2 if part else steps * (step >= steps // 2))

    whole = pl.BlockSpec((2, row_count, dim), lambda i, meta: (0, 0, 0))
    return pl.pallas_call(
        functools.partial(attend_kernel, tile, block_of),
        grid_spec=pltpu.PrefetchScalarGridSpec(
            num_scalar_prefetch=1,
            grid=(steps,),
            in_specs=[whole] * 2
            + [pl.BlockSpec((query.shape[0], tile, dim), lambda i, meta: (0, block_of(i), 0)) for query in queries],
            out_specs=pl.BlockSpec((tile, heads * dim), lambda i, meta: (i, 0)),
            scratch_shapes=[
                pltpu.VMEM((2 * row_count, dim), jnp.bfloat16),
                pltpu.VMEM((2 * row_count, 2 * dim), jnp.bfloat16),
                pltpu.VMEM((heads, tile, 2 * dim), jnp.float32),
            ],
        ),
        out_shape=jax.ShapeDtypeStruct((steps * tile, heads * dim), jnp.bfloat16),
        compiler_params=pltpu.CompilerParams(vmem_limit_bytes=VMEM_LIMIT),
        cost_estimate=pl.CostEstimate(
            flops=8 * heads * row_count * row_count * dim, bytes_accessed=4 * row_count * dim, transcendentals=0
        ),
    )(meta, own, far, *queries)


def output_kernel(plan, meta, kept_rows, sent_rows, *rest):
    *shards, kept, sent = rest
    columns = shards[0].shape[1]
    for index, pieces in enumerate(plan):
        here = pl.ds(pl.multiple_of(meta[index] * columns, columns), columns)
        for rows, out in ((kept_rows, kept), (sent_rows, sent)):
            product = 0.0
            for shard, start, size, depth in pieces:
                left = rows[:, depth : depth + size]
                right = shards[shard][start : start + size, :]
                product += jnp.dot(left, right, preferred_element_type=jnp.float32)
            out[:, :, here] = product.astype(jnp.bfloat16).reshape(*out.shape[:2], columns)


def output_part(plan, meta, kept_rows, sent_rows, tile, shards):
    count, depth = kept_rows.shape
    width = len(plan) * shards[0].shape[1]

    def whole(shape):
        return pl.BlockSpec(shape, lambda n, meta: (0,) * len(shape))

    out = (count // 2 // tile, tile, width)
    return pl.pallas_call(
        functools.partial(output_kernel, plan),
        grid_spec=pltpu.PrefetchScalarGridSpec(
            num_scalar_prefetch=1,
            grid=(1,),
            in_specs=[pl.BlockSpec((count // 2, depth), lambda n, meta, half=half: (half, 0)) for half in range(2)]
            + [whole(shard.shape) for shard in shards],
            out_specs=[whole(out)] * 2,
        ),
        out_shape=[jax.ShapeDtypeStruct(out, jnp.bfloat16)] * 2,
        compiler_params=pltpu.CompilerParams(vmem_limit_bytes=VMEM_LIMIT),
        cost_estimate=pl.CostEstimate(flops=6 * count * width * depth, bytes_accessed=4 * count * width, transcendentals=0),
    )(meta, kept_rows, sent_rows, *shards)


def finish_kernel(states, gain, *rest):
    *terms, hidden_out, normed_out = rest
    total = functools.reduce(jnp.add, [term[...].astype(jnp.float32) for term in terms])
    rounded = (states[...].astype(jnp.float32) + total).astype(jnp.bfloat16)
    hidden_out[...] = rounded
    hidden = rounded.astype(jnp.float32)
    inverse = lax.rsqrt(jnp.mean(hidden * hidden, axis=-1, keepdims=True) + epsilon)
    normed_out[...] = (hidden * inverse * gain[...]).astype(jnp.bfloat16)


def finish(states, gain, terms):
    rows, width = states.shape
    tile = min(64, rows)
    block = pl.BlockSpec((tile, width), lambda i: (i, 0))
    return pl.pallas_call(
        finish_kernel,
        grid=(rows // tile,),
        in_specs=[block, pl.BlockSpec((1, width), lambda i: (0, 0))] + [block] * len(terms),
        out_specs=[block] * 2,
        out_shape=[jax.ShapeDtypeStruct((rows, width), jnp.bfloat16)] * 2,
        compiler_params=pltpu.CompilerParams(vmem_limit_bytes=VMEM_LIMIT),
        cost_estimate=FREE,
    )(states, gain[None, :], *terms)


def per_device(
    hidden_in,
    norm_attention,
    norm_experts,
    query_master,
    trainer_key_value_weight,
    output_master,
    query_gain,
    key_gain,
    lengths,
    router,
    expert_gateup,
    expert_down,
    routes,
):
    experts_axis = lax.axis_size("expert")
    group_member = lax.axis_index("expert")
    group_index = lax.axis_index("group")
    heads = QUERY_HEADS // experts_axis
    dim = HEAD_DIMENSION
    rows_here, model_width = hidden_in.shape
    local_rows = rows_here * experts_axis

    groups = lax.axis_size("group")
    place, side = group_index // 2, group_index % 2
    common_head = group_member * heads // (QUERY_HEADS // KEY_VALUE_HEADS)
    joined = pack(common_head.astype(jnp.int32).reshape(1), query_master, trainer_key_value_weight)
    output_here = output_master.astype(jnp.bfloat16)
    joined_rounds = Beside(joined)
    normed = norm_rows(after(hidden_in, joined), norm_attention).astype(jnp.bfloat16)
    blocks = gather_tokens(normed)
    parity = after(side, joined_rounds.token())
    output_here = after(output_here, joined_rounds.token())
    output_crossed = cross(output_here)
    joined_rounds.round()
    query_gain, key_gain, lengths, routes = lax.optimization_barrier(
        (query_gain, key_gain, lengths, routes, joined_rounds.token())
    )[:4]
    joined_rounds.round()
    output_here, output_crossed = lax.optimization_barrier(
        (output_here, output_crossed, joined_rounds.token())
    )[:2]
    depth = output_here.shape[0]
    if groups == 8:
        first = depth // 4
        rest = depth - first
        output_block = jnp.concatenate([output_here[:first], output_crossed[:first], output_here[first:]], axis=0)
        output_rounds = Beside(output_block, output_crossed[first:], 2 * first)
        plan = [((k, 0, first, 0), (k, 2 * first, rest, first)) for k in range(4)]
        plan += [((k, first, first, 0), (4 + k, 0, rest, first)) for k in range(4)]
    else:
        output_rounds = Beside(output_here)
        plan = [((k, 0, depth, 0),) for k in range(groups)]
    joined_rounds.round()
    shards = joined_rounds.held(range(groups))
    output_rounds.round(joined_rounds.token())

    masks = doubling_masks(experts_axis)
    block_order = jnp.bitwise_xor(group_member, jnp.array(masks, jnp.int32))
    meta = jnp.concatenate([jnp.stack([place, side]), held_groups(place, side), block_order]).astype(jnp.int32)

    inside = routes < experts_axis
    expert_window = jnp.sum(jnp.where(inside, routes, 0), axis=1)
    present = jnp.any(inside, axis=1)
    capacity = local_rows // (experts_axis * experts_axis)
    member_table = (present[:, None] & (expert_window[:, None] == block_order[None, :])).astype(jnp.int32)
    ranking = jnp.cumsum(member_table, axis=0) - 1
    slot_index = jnp.sum(member_table * (ranking + jnp.arange(experts_axis) * capacity), axis=1)
    select = (
        (jnp.arange(experts_axis * capacity)[:, None] == slot_index[None, :]) & present[None, :]
    ).astype(jnp.bfloat16)

    own_places = local_positions(parity, local_rows).astype(jnp.float32)
    exponents = jnp.arange(dim // 2).astype(jnp.float32)
    inverse = jnp.exp(exponents * (-2.0 * math.log(rope_theta) / dim))
    angles = own_places[:, None] * inverse[None, :]
    cosine_values, sine_values = jnp.cos(angles), jnp.sin(angles)
    cosine = jnp.concatenate([cosine_values, cosine_values], axis=1)
    sine = jnp.concatenate([-sine_values, sine_values], axis=1)

    def tables(gain):
        return cosine * gain, sine * jnp.roll(gain, dim // 2)

    lanes = jnp.arange(dim)
    swap = (lanes[:, None] == (lanes[None, :] + dim // 2) % dim).astype(jnp.float32)
    nothing = jnp.zeros((dim, dim), jnp.float32)
    mixer = jnp.block([[swap, nothing], [nothing, nothing + 1.0 / dim]]).astype(jnp.bfloat16)
    query_tables = tables(query_gain * (dim**-0.5 * math.log2(math.e)))
    key_tables = tables(key_gain)
    blocks[0] = after(blocks[0], select)
    own_pair = project(key_kernel, 0, 1, meta, blocks, shards, *key_tables, mixer)
    far_pair = cross(own_pair)
    rows_now = [after(blocks[0], own_pair)] + blocks[1:]
    queries = [project(query_kernel, 1, heads // 2, meta, rows_now, shards, *query_tables, mixer)]
    queries[0] = after(queries[0], output_rounds.token())
    output_rounds.round(queries[0], far_pair)

    valid_length = jnp.sum(jnp.where(jnp.arange(lengths.shape[0]) == group_index // 2, lengths, 0))
    attend_meta = jnp.concatenate([jnp.stack([parity, valid_length]), block_order]).astype(jnp.int32)
    outer_rows = attend(attend_meta, queries, own_pair, far_pair, rows_here, 0)
    queries[0] = after(queries[0], output_rounds.token())
    output_rounds.round(outer_rows)
    inner_rows = attend(attend_meta, queries, own_pair, far_pair, rows_here, 1)

    output_shards = output_rounds.held(range(groups))
    output_meta = held_groups(place, side).astype(jnp.int32)
    kept, sent = output_part(plan, output_meta, inner_rows, outer_rows, rows_here, output_shards)
    next_sum = sum_terms([kept, from_xor(sent, "expert", 1)])
    kept, sent = output_part(plan, output_meta, outer_rows, inner_rows, rows_here, output_shards)
    terms = scatter_rest([kept, from_xor(sent, "expert", 1)], next_sum)
    hidden, normed_second = finish(hidden_in, norm_experts, terms)

    logits = jnp.dot(normed_second, router, preferred_element_type=jnp.float32)
    route_table = routes[:, :, None] == jnp.arange(logits.shape[1])[None, None, :]
    picked = jnp.sum(jnp.where(route_table, logits[:, None, :], 0.0), axis=-1)
    raised = jnp.exp(picked)
    gate_values = raised / jnp.sum(raised, axis=1, keepdims=True)
    gate_window = jnp.sum(jnp.where(inside, gate_values, 0.0), axis=1)
    outgoing = (
        jnp.dot(select, normed_second, preferred_element_type=jnp.float32)
        .astype(jnp.bfloat16)
        .reshape(experts_axis, capacity, model_width)
    )

    gateup_here = expert_gateup[0]
    down_here = expert_down[0]
    hidden_units = down_here.shape[0]

    def expert(slots):
        gate_up = jnp.dot(slots, gateup_here, preferred_element_type=jnp.float32)
        active = (jax.nn.silu(gate_up[:, :hidden_units]) * gate_up[:, hidden_units:]).astype(jnp.bfloat16)
        return jnp.dot(active, down_here, preferred_element_type=jnp.float32).astype(jnp.bfloat16)

    far = [j for j in range(experts_axis) if masks[j] >= experts_axis // 2]
    first, second = far[: len(far) // 2], far[len(far) // 2 :]
    near = [j for j in range(1, experts_axis) if j not in far]
    results = {}
    arrived = {j: from_xor(outgoing[j], "expert", masks[j]) for j in first}
    held = after(outgoing, *arrived.values())
    arrived.update({j: from_xor(held[j], "expert", masks[j]) for j in second + near})
    arrived[0] = outgoing[0]
    for part in (first, second + near + [0]):
        done = expert(jnp.concatenate([arrived[j] for j in part], axis=0))
        for index, j in enumerate(part):
            results[j] = done[index * capacity : (index + 1) * capacity]
    returned = jnp.stack(
        [results[0]] + [from_xor(results[j], "expert", masks[j]) for j in range(1, experts_axis)]
    )
    combined = jnp.dot(
        jnp.transpose(select), returned.reshape(-1, model_width), preferred_element_type=jnp.float32
    )
    expert_mix = (gate_window[:, None] * combined).astype(jnp.bfloat16)
    return (hidden, expert_mix)


def solution(mesh):
    return jax.shard_map(
        per_device,
        mesh=mesh,
        in_specs=(
            P(("group", "expert"), None),
            P(),
            P(),
            P("group", "expert"),
            P(None, "group", None),
            P("expert", "group"),
            P(),
            P(),
            P(),
            P(),
            P("expert", None, None),
            P("expert", None, None),
            P(("group", "expert"), None),
        ),
        out_specs=(P(("group", "expert"), None), P(("group", "expert"), None)),
        check_vma=False,
    )
```

```python
import functools
import math

import jax
import jax.numpy as jnp
from jax import lax
from jax.experimental import pallas as pl
from jax.experimental.pallas import tpu as pltpu
from jax.sharding import PartitionSpec as P

QUERY_HEADS = 32
KEY_VALUE_HEADS = 4
HEAD_DIMENSION = 128

epsilon = 1e-06
rope_theta = 1000000.0
VMEM_LIMIT = 32 * 1024 * 1024
FREE = pl.CostEstimate(flops=0, bytes_accessed=0, transcendentals=0)


def norm_rows(values, gain_vector):
    widened = values.astype(jnp.float32)
    inverse_rms = lax.rsqrt(jnp.mean(widened * widened, axis=-1, keepdims=True) + epsilon)
    return widened * inverse_rms * gain_vector


def local_positions(parity, row_count):
    indices = jnp.arange(row_count)
    quarter = row_count // 2
    offset = jnp.where(parity == 0, jnp.where(indices < quarter, 0, 2 * quarter), quarter)
    return indices + offset


def from_xor(block, axis, mask):
    count = lax.axis_size(axis)
    return lax.ppermute(block, axis, [(i, i ^ mask) for i in range(count)])


def cross(block):
    return from_xor(block, "group", 1)


def after(block, *others):
    return lax.optimization_barrier((block, *others))[0]


LINE = ((0, 1, 2, 3), (1, 0, 2, 3), (2, 3, 1, 0), (3, 2, 1, 0))
PAIRS = ((0, 1), (1, 0), (2, 3), (3, 2))
MIDDLE = ((1, 2), (2, 1))
OUTWARD = ((1, 0), (2, 3))


def along(block, moves):
    return lax.ppermute(block, "group", [(2 * a + s, 2 * b + s) for a, b in moves for s in range(2)])


def line_rounds(block, shards, crossed, head):
    place = lax.axis_index("group") // 2
    edge = (place == 0) | (place == 3)
    shards[0] = block
    if crossed is None:
        shards[1], inner, shards[4] = yield along(block, PAIRS), along(block, MIDDLE), cross(block[head:])
    else:
        shards[4] = crossed
        shards[1], inner = yield along(block, PAIRS), along(block, MIDDLE)
    shards[5], inner_far, outer = yield cross(shards[1][head:]), along(shards[1], MIDDLE), along(inner, OUTWARD)
    shards[2] = jnp.where(edge, outer, inner)
    shards[6], outer = yield cross(shards[2][head:]), along(inner_far, OUTWARD)
    shards[3] = jnp.where(edge, outer, inner_far)
    (shards[7],) = yield (cross(shards[3][head:]),)
    yield ()


class Beside:
    def __init__(self, block, crossed=None, head=0):
        groups = lax.axis_size("group")
        self.found = [None] * groups if groups == 8 else list(lax.all_gather(block, "group"))
        self.chain = line_rounds(block, self.found, crossed, head) if groups == 8 else None
        self.brought = (block,) if self.chain is None else lax.optimization_barrier(next(self.chain))

    def round(self, *ready):
        if self.chain is not None:
            results = after(self.brought, *ready)
            self.brought = lax.optimization_barrier(self.chain.send(results))

    def token(self):
        return self.brought[0]

    def held(self, indices):
        if self.chain is not None and any(self.found[index] is None for index in indices):
            self.chain.send(self.brought)
            self.chain = None
        return [self.found[index] for index in indices]


def held_groups(place, side):
    groups = lax.axis_size("group")
    if groups != 8:
        return jnp.arange(groups)
    places = jnp.sum(jnp.where(jnp.arange(4)[:, None] == place, jnp.array(LINE, jnp.int32), 0), axis=0)
    return jnp.concatenate([2 * places + side, 2 * places + 1 - side])


def doubling_masks(count):
    masks, stride = [0], count // 2
    while stride:
        masks = masks + [mask ^ stride for mask in masks]
        stride //= 2
    return masks


def gather_tokens(rows):
    blocks = [rows]
    stride = lax.axis_size("expert") // 2
    while stride:
        blocks = blocks + [from_xor(block, "expert", stride) for block in blocks]
        stride //= 2
    return blocks


def sum_terms(terms):
    return functools.reduce(jnp.add, [term.astype(jnp.float32) for term in terms]).astype(jnp.bfloat16)


def scatter_rest(kept, sent):
    stride = 2
    while True:
        kept = [*kept, from_xor(sent, "expert", stride)]
        half = sent.shape[0] // 2
        if not half:
            return [term[0] for term in kept]
        whole = sum_terms(kept)
        kept, sent = [whole[:half]], whole[half:]
        stride *= 2


def stack_shards(meta, refs, weights):
    depth = weights.shape[0] // len(refs)
    for index, ref in enumerate(refs):
        weights[pl.ds(pl.multiple_of(meta[2 + index] * depth, depth), depth), :] = ref[...]


def pack_kernel(meta, query, pair, out):
    dim = HEAD_DIMENSION
    out[:, :dim] = pair[0].astype(jnp.bfloat16)
    out[:, dim : 2 * dim] = pair[1].astype(jnp.bfloat16)
    out[:, 2 * dim :] = query[...].astype(jnp.bfloat16)


def pack(head, query, pair):
    rows, columns = query.shape
    dim = HEAD_DIMENSION
    tile = min(64, rows)
    return pl.pallas_call(
        pack_kernel,
        grid_spec=pltpu.PrefetchScalarGridSpec(
            num_scalar_prefetch=1,
            grid=(rows // tile,),
            in_specs=[
                pl.BlockSpec((tile, columns), lambda i, meta: (i, 0)),
                pl.BlockSpec((2, tile, dim), lambda i, meta: (0, i, meta[0])),
            ],
            out_specs=pl.BlockSpec((tile, columns + 2 * dim), lambda i, meta: (i, 0)),
        ),
        out_shape=jax.ShapeDtypeStruct((rows, columns + 2 * dim), jnp.bfloat16),
        compiler_params=pltpu.CompilerParams(vmem_limit_bytes=VMEM_LIMIT),
        cost_estimate=FREE,
    )(head, query, pair)


def turn(values, cosines, sines, mixer):
    values = values.astype(jnp.bfloat16)
    wide = values.astype(jnp.float32)
    both = jnp.concatenate([values, (wide * wide).astype(jnp.bfloat16)], axis=1)
    mixed = jnp.dot(both, mixer, preferred_element_type=jnp.float32)
    dim = values.shape[1]
    inverse = lax.rsqrt(mixed[:, dim:] + epsilon)
    return ((wide * cosines + mixed[:, :dim] * sines) * inverse).astype(jnp.bfloat16)


def query_kernel(count, meta, *rest):
    rows, (cosine, sine, mixer, *rest) = rest[:count], rest[count:]
    *shards, query_out, weights, joined = rest
    stack_shards(meta, shards, weights)
    tile, dim = rows[0].shape[0], HEAD_DIMENSION

    @pl.when(pl.program_id(0) == 0)
    def _():
        for index, block in enumerate(rows):
            joined[index * tile : (index + 1) * tile, :] = block[...]

    projected = jnp.dot(joined[...], weights[...], preferred_element_type=jnp.float32)
    for block in range(count):
        spot = pl.ds(pl.multiple_of(meta[2 + len(shards) + block] * tile, tile), tile)
        here = slice(block * tile, (block + 1) * tile)
        for head in range(2):
            query_out[head, here, :] = turn(
                projected[here, head * dim : (head + 1) * dim], cosine[spot, :], sine[spot, :], mixer[...]
            )


def key_kernel(count, meta, *rest):
    rows, (cosine, sine, mixer, *rest) = rest[:count], rest[count:]
    *shards, pair_out, weights, joined = rest
    stack_shards(meta, shards, weights)
    tile, dim = rows[0].shape[0], HEAD_DIMENSION

    @pl.when(pl.program_id(0) == 0)
    def _():
        for index, block in enumerate(rows):
            joined[index * tile : (index + 1) * tile, :] = block[...]

    projected = jnp.dot(joined[...], weights[...], preferred_element_type=jnp.float32)
    for block in range(count):
        spot = pl.ds(pl.multiple_of(meta[2 + len(shards) + block] * tile, tile), tile)
        here = slice(block * tile, (block + 1) * tile)
        pair_out[0, spot, :] = turn(projected[here, :dim], cosine[spot, :], sine[spot, :], mixer[...])
        pair_out[1, spot, :] = projected[here, dim:].astype(jnp.bfloat16)


def project(kernel, first, steps, meta, blocks, shards, cosine, sine, mixer):
    count, (tile, width) = len(blocks), blocks[0].shape
    dim = HEAD_DIMENSION
    shard = pl.BlockSpec((shards[0].shape[0], 2 * dim), lambda n, meta: (0, first + n))
    table = pl.BlockSpec((count * tile, dim), lambda n, meta: (0, 0))
    return pl.pallas_call(
        functools.partial(kernel, count),
        grid_spec=pltpu.PrefetchScalarGridSpec(
            num_scalar_prefetch=1,
            grid=(steps,),
            in_specs=[pl.BlockSpec((tile, width), lambda n, meta: (0, 0))] * count
            + [
                table,
                table,
                pl.BlockSpec((2 * dim, 2 * dim), lambda n, meta: (0, 0)),
            ]
            + [shard] * len(shards),
            out_specs=pl.BlockSpec((2, count * tile, dim), lambda n, meta: (n, 0, 0)),
            scratch_shapes=[
                pltpu.VMEM((width, 2 * dim), jnp.bfloat16),
                pltpu.VMEM((count * tile, width), jnp.bfloat16),
            ],
        ),
        out_shape=jax.ShapeDtypeStruct((2 * steps, count * tile, dim), jnp.bfloat16),
        compiler_params=pltpu.CompilerParams(vmem_limit_bytes=VMEM_LIMIT),
        cost_estimate=pl.CostEstimate(
            flops=16 * steps * count * tile * width * dim, bytes_accessed=2 * count * tile * width, transcendentals=0
        ),
    )(meta, *blocks, cosine, sine, mixer, *shards)


def attend_kernel(tile, block_of, meta, own, far, *rest):
    *queries, out, keys, values, total = rest
    heads, dim = total.shape[0], HEAD_DIMENSION
    query = [part.at[head] for part in queries for head in range(part.shape[0])]
    row_count = own.shape[1]
    half = row_count // 2
    parity, length = meta[0], meta[1]
    step = pl.program_id(0)

    @pl.when(step == 0)
    def _():
        ones = jnp.ones((half, dim), jnp.bfloat16)
        for pair, whose in ((own, parity), (far, 1 - parity)):
            for part in range(2):
                base = jnp.where(whose == 0, 3 * half * part, half * (1 + part))
                base = pl.multiple_of(base, half)
                source = pl.ds(part * half, half)
                keys[pl.ds(base, half), :] = pair[0, source, :]
                valid = base + lax.broadcasted_iota(jnp.int32, (half, dim), 0) < length
                zero = jnp.zeros((half, dim), jnp.bfloat16)
                values[pl.ds(base, half), :dim] = jnp.where(valid, pair[1, source, :], zero)
                values[pl.ds(base, half), dim:] = jnp.where(valid, ones, zero)

    first = meta[2 + block_of(step)] * tile
    first = first + jnp.where(parity == 0, jnp.where(first < half, 0, 2 * half), half)

    def weigh(head, start, width, masked):
        scores = lax.dot_general(
            query[head][...], keys[pl.ds(start, width), :], (((1,), (1,)), ((), ())),
            preferred_element_type=jnp.float32,
        )
        weights = jnp.exp2(scores)
        if masked:
            below = lax.broadcasted_iota(jnp.int32, weights.shape, 1) <= lax.broadcasted_iota(
                jnp.int32, weights.shape, 0
            )
            weights = jnp.where(below, weights, 0.0)
        return jnp.dot(
            weights.astype(jnp.bfloat16), values[pl.ds(start, width), :], preferred_element_type=jnp.float32
        )

    diagonal = pl.multiple_of(first, tile)
    for head in range(heads):
        total[head] = weigh(head, diagonal, tile, True)

    def wide(index, _):
        start = pl.multiple_of(index * half, half)
        for head in range(heads):
            total[head] += weigh(head, start, half, False)
        return 0

    lax.fori_loop(0, first // half, wide, 0)

    def narrow(index, _):
        start = pl.multiple_of(index * tile, tile)
        for head in range(heads):
            total[head] += weigh(head, start, tile, False)
        return 0

    lax.fori_loop(first // half * (half // tile), first // tile, narrow, 0)
    for head in range(heads):
        summed = total[head]
        out[:, head * dim : (head + 1) * dim] = (summed[:, :dim] / summed[:, dim:]).astype(jnp.bfloat16)


def attend(meta, queries, own, far, tile, part):
    _, row_count, dim = queries[0].shape
    heads = sum(query.shape[0] for query in queries)
    steps = row_count // tile // 2

    def block_of(step):
        return step + (steps // 2 if part else steps * (step >= steps // 2))

    whole = pl.BlockSpec((2, row_count, dim), lambda i, meta: (0, 0, 0))
    return pl.pallas_call(
        functools.partial(attend_kernel, tile, block_of),
        grid_spec=pltpu.PrefetchScalarGridSpec(
            num_scalar_prefetch=1,
            grid=(steps,),
            in_specs=[whole] * 2
            + [pl.BlockSpec((query.shape[0], tile, dim), lambda i, meta: (0, block_of(i), 0)) for query in queries],
            out_specs=pl.BlockSpec((tile, heads * dim), lambda i, meta: (i, 0)),
            scratch_shapes=[
                pltpu.VMEM((2 * row_count, dim), jnp.bfloat16),
                pltpu.VMEM((2 * row_count, 2 * dim), jnp.bfloat16),
                pltpu.VMEM((heads, tile, 2 * dim), jnp.float32),
            ],
        ),
        out_shape=jax.ShapeDtypeStruct((steps * tile, heads * dim), jnp.bfloat16),
        compiler_params=pltpu.CompilerParams(vmem_limit_bytes=VMEM_LIMIT),
        cost_estimate=pl.CostEstimate(
            flops=8 * heads * row_count * row_count * dim, bytes_accessed=4 * row_count * dim, transcendentals=0
        ),
    )(meta, own, far, *queries)


def output_kernel(plan, meta, kept_rows, sent_rows, *rest):
    *shards, kept, sent = rest
    columns = shards[0].shape[1]
    for index, pieces in enumerate(plan):
        here = pl.ds(pl.multiple_of(meta[index] * columns, columns), columns)
        for rows, out in ((kept_rows, kept), (sent_rows, sent)):
            product = 0.0
            for shard, start, size, depth in pieces:
                left = rows[:, depth : depth + size]
                right = shards[shard][start : start + size, :]
                product += jnp.dot(left, right, preferred_element_type=jnp.float32)
            out[:, :, here] = product.astype(jnp.bfloat16).reshape(*out.shape[:2], columns)


def output_part(plan, meta, kept_rows, sent_rows, tile, shards):
    count, depth = kept_rows.shape
    width = len(plan) * shards[0].shape[1]

    def whole(shape):
        return pl.BlockSpec(shape, lambda n, meta: (0,) * len(shape))

    out = (count // 2 // tile, tile, width)
    return pl.pallas_call(
        functools.partial(output_kernel, plan),
        grid_spec=pltpu.PrefetchScalarGridSpec(
            num_scalar_prefetch=1,
            grid=(1,),
            in_specs=[pl.BlockSpec((count // 2, depth), lambda n, meta, half=half: (half, 0)) for half in range(2)]
            + [whole(shard.shape) for shard in shards],
            out_specs=[whole(out)] * 2,
        ),
        out_shape=[jax.ShapeDtypeStruct(out, jnp.bfloat16)] * 2,
        compiler_params=pltpu.CompilerParams(vmem_limit_bytes=VMEM_LIMIT),
        cost_estimate=pl.CostEstimate(flops=6 * count * width * depth, bytes_accessed=4 * count * width, transcendentals=0),
    )(meta, kept_rows, sent_rows, *shards)


def finish_kernel(states, gain, *rest):
    *terms, hidden_out, normed_out = rest
    total = functools.reduce(jnp.add, [term[...].astype(jnp.float32) for term in terms])
    rounded = (states[...].astype(jnp.float32) + total).astype(jnp.bfloat16)
    hidden_out[...] = rounded
    hidden = rounded.astype(jnp.float32)
    inverse = lax.rsqrt(jnp.mean(hidden * hidden, axis=-1, keepdims=True) + epsilon)
    normed_out[...] = (hidden * inverse * gain[...]).astype(jnp.bfloat16)


def finish(states, gain, terms):
    rows, width = states.shape
    tile = min(64, rows)
    block = pl.BlockSpec((tile, width), lambda i: (i, 0))
    return pl.pallas_call(
        finish_kernel,
        grid=(rows // tile,),
        in_specs=[block, pl.BlockSpec((1, width), lambda i: (0, 0))] + [block] * len(terms),
        out_specs=[block] * 2,
        out_shape=[jax.ShapeDtypeStruct((rows, width), jnp.bfloat16)] * 2,
        compiler_params=pltpu.CompilerParams(vmem_limit_bytes=VMEM_LIMIT),
        cost_estimate=FREE,
    )(states, gain[None, :], *terms)


def per_device(
    hidden_in,
    norm_attention,
    norm_experts,
    query_master,
    trainer_key_value_weight,
    output_master,
    query_gain,
    key_gain,
    lengths,
    router,
    expert_gateup,
    expert_down,
    routes,
):
    experts_axis = lax.axis_size("expert")
    group_member = lax.axis_index("expert")
    group_index = lax.axis_index("group")
    heads = QUERY_HEADS // experts_axis
    dim = HEAD_DIMENSION
    rows_here, model_width = hidden_in.shape
    local_rows = rows_here * experts_axis

    groups = lax.axis_size("group")
    place, side = group_index // 2, group_index % 2
    common_head = group_member * heads // (QUERY_HEADS // KEY_VALUE_HEADS)
    joined = pack(common_head.astype(jnp.int32).reshape(1), query_master, trainer_key_value_weight)
    output_here = output_master.astype(jnp.bfloat16)
    joined_rounds = Beside(joined)
    normed = norm_rows(after(hidden_in, joined), norm_attention).astype(jnp.bfloat16)
    blocks = gather_tokens(normed)
    parity = after(side, joined_rounds.token())
    output_here = after(output_here, joined_rounds.token())
    output_crossed = cross(output_here)
    joined_rounds.round()
    query_gain, key_gain, lengths, routes = lax.optimization_barrier(
        (query_gain, key_gain, lengths, routes, joined_rounds.token())
    )[:4]
    joined_rounds.round()
    output_here, output_crossed = lax.optimization_barrier(
        (output_here, output_crossed, joined_rounds.token())
    )[:2]
    depth = output_here.shape[0]
    if groups == 8:
        first = depth // 4
        rest = depth - first
        output_block = jnp.concatenate([output_here[:first], output_crossed[:first], output_here[first:]], axis=0)
        output_rounds = Beside(output_block, output_crossed[first:], 2 * first)
        plan = [((k, 0, first, 0), (k, 2 * first, rest, first)) for k in range(4)]
        plan += [((k, first, first, 0), (4 + k, 0, rest, first)) for k in range(4)]
    else:
        output_rounds = Beside(output_here)
        plan = [((k, 0, depth, 0),) for k in range(groups)]
    joined_rounds.round()
    shards = joined_rounds.held(range(groups))
    output_rounds.round()

    masks = doubling_masks(experts_axis)
    block_order = jnp.bitwise_xor(group_member, jnp.array(masks, jnp.int32))
    meta = jnp.concatenate([jnp.stack([place, side]), held_groups(place, side), block_order]).astype(jnp.int32)

    inside = routes < experts_axis
    expert_window = jnp.sum(jnp.where(inside, routes, 0), axis=1)
    present = jnp.any(inside, axis=1)
    capacity = local_rows // (experts_axis * experts_axis)
    member_table = (present[:, None] & (expert_window[:, None] == block_order[None, :])).astype(jnp.int32)
    ranking = jnp.cumsum(member_table, axis=0) - 1
    slot_index = jnp.sum(member_table * (ranking + jnp.arange(experts_axis) * capacity), axis=1)
    select = (
        (jnp.arange(experts_axis * capacity)[:, None] == slot_index[None, :]) & present[None, :]
    ).astype(jnp.bfloat16)

    own_places = local_positions(parity, local_rows).astype(jnp.float32)
    exponents = jnp.arange(dim // 2).astype(jnp.float32)
    inverse = jnp.exp(exponents * (-2.0 * math.log(rope_theta) / dim))
    angles = own_places[:, None] * inverse[None, :]
    cosine_values, sine_values = jnp.cos(angles), jnp.sin(angles)
    cosine = jnp.concatenate([cosine_values, cosine_values], axis=1)
    sine = jnp.concatenate([-sine_values, sine_values], axis=1)

    def tables(gain):
        return cosine * gain, sine * jnp.roll(gain, dim // 2)

    lanes = jnp.arange(dim)
    swap = (lanes[:, None] == (lanes[None, :] + dim // 2) % dim).astype(jnp.float32)
    nothing = jnp.zeros((dim, dim), jnp.float32)
    mixer = jnp.block([[swap, nothing], [nothing, nothing + 1.0 / dim]]).astype(jnp.bfloat16)
    query_tables = tables(query_gain * (dim**-0.5 * math.log2(math.e)))
    key_tables = tables(key_gain)
    blocks[0] = after(blocks[0], select)
    own_pair = project(key_kernel, 0, 1, meta, blocks, shards, *key_tables, mixer)
    far_pair = cross(own_pair)
    rows_now = [after(blocks[0], own_pair, output_rounds.token())] + blocks[1:]
    output_rounds.round(own_pair)
    queries = [project(query_kernel, 1, heads // 2, meta, rows_now, shards, *query_tables, mixer)]

    valid_length = jnp.sum(jnp.where(jnp.arange(lengths.shape[0]) == group_index // 2, lengths, 0))
    attend_meta = jnp.concatenate([jnp.stack([parity, valid_length]), block_order]).astype(jnp.int32)
    outer_rows = attend(attend_meta, queries, own_pair, far_pair, rows_here, 0)
    queries[0] = after(queries[0], output_rounds.token())
    output_rounds.round(outer_rows)
    inner_rows = attend(attend_meta, queries, own_pair, far_pair, rows_here, 1)

    output_shards = output_rounds.held(range(groups))
    output_meta = held_groups(place, side).astype(jnp.int32)
    kept, sent = output_part(plan, output_meta, inner_rows, outer_rows, rows_here, output_shards)
    next_sum = sum_terms([kept, from_xor(sent, "expert", 1)])
    kept, sent = output_part(plan, output_meta, outer_rows, inner_rows, rows_here, output_shards)
    terms = scatter_rest([kept, from_xor(sent, "expert", 1)], next_sum)
    hidden, normed_second = finish(hidden_in, norm_experts, terms)

    logits = jnp.dot(normed_second, router, preferred_element_type=jnp.float32)
    route_table = routes[:, :, None] == jnp.arange(logits.shape[1])[None, None, :]
    picked = jnp.sum(jnp.where(route_table, logits[:, None, :], 0.0), axis=-1)
    raised = jnp.exp(picked)
    gate_values = raised / jnp.sum(raised, axis=1, keepdims=True)
    gate_window = jnp.sum(jnp.where(inside, gate_values, 0.0), axis=1)
    outgoing = (
        jnp.dot(select, normed_second, preferred_element_type=jnp.float32)
        .astype(jnp.bfloat16)
        .reshape(experts_axis, capacity, model_width)
    )

    gateup_here = expert_gateup[0]
    down_here = expert_down[0]
    hidden_units = down_here.shape[0]

    def expert(slots):
        gate_up = jnp.dot(slots, gateup_here, preferred_element_type=jnp.float32)
        active = (jax.nn.silu(gate_up[:, :hidden_units]) * gate_up[:, hidden_units:]).astype(jnp.bfloat16)
        return jnp.dot(active, down_here, preferred_element_type=jnp.float32).astype(jnp.bfloat16)

    far = [j for j in range(experts_axis) if masks[j] >= experts_axis // 2]
    first, second = far[: len(far) // 2], far[len(far) // 2 :]
    near = [j for j in range(1, experts_axis) if j not in far]
    results = {}
    arrived = {j: from_xor(outgoing[j], "expert", masks[j]) for j in first}
    held = after(outgoing, *arrived.values())
    arrived.update({j: from_xor(held[j], "expert", masks[j]) for j in second + near})
    arrived[0] = outgoing[0]
    for part in (first, second + near + [0]):
        done = expert(jnp.concatenate([arrived[j] for j in part], axis=0))
        for index, j in enumerate(part):
            results[j] = done[index * capacity : (index + 1) * capacity]
    returned = jnp.stack(
        [results[0]] + [from_xor(results[j], "expert", masks[j]) for j in range(1, experts_axis)]
    )
    combined = jnp.dot(
        jnp.transpose(select), returned.reshape(-1, model_width), preferred_element_type=jnp.float32
    )
    expert_mix = (gate_window[:, None] * combined).astype(jnp.bfloat16)
    return (hidden, expert_mix)


def solution(mesh):
    return jax.shard_map(
        per_device,
        mesh=mesh,
        in_specs=(
            P(("group", "expert"), None),
            P(),
            P(),
            P("group", "expert"),
            P(None, "group", None),
            P("expert", "group"),
            P(),
            P(),
            P(),
            P(),
            P("expert", None, None),
            P("expert", None, None),
            P(("group", "expert"), None),
        ),
        out_specs=(P(("group", "expert"), None), P(("group", "expert"), None)),
        check_vma=False,
    )
```
